32 devices in a mesh: rep: 2 (over y), ctx: 4 (over z), ep: 4 (over x, core), tp: 1.
Axes of the slice: x: 2, y: 2, z: 4, core: 2. Of those that a mesh axis runs over, the one named last changes fastest.
Arguments:
- queries: bfloat16 [512, 2, 16, 128], P(('rep', 'ctx'), 'tp', 'ep'), parts along dimension 0, may hold values from -120 to 120
- key_rows: bfloat16 [1024, 2, 128], P(('rep', 'ctx'), 'tp'), parts along dimension 0, may hold values from -6.5 to 6.5
- values: bfloat16 [1024, 2, 128], P(('rep', 'ctx'), 'tp'), parts along dimension 0, may hold values from -48 to 48
- offset: int32 [2], P('rep'), parts along dimension 0, may hold values from 0 to 256
- tokens: bfloat16 [4096, 2048], P(('rep', 'ctx', 'ep')), parts along dimension 0, may hold values from -6 to 6
- routes: int32 [4096, 8], P(('rep', 'ctx', 'ep')), parts along dimension 0, may hold values from 0 to 15, all different within a row; in each aligned block of 128 rows (0 to 127, 128 to 255, ...) at most 80 rows name the same one
- gate_share: float32 [4096, 8], P(('rep', 'ctx', 'ep')), parts along dimension 0, may hold values from 0.1 to 1
- expert_gate: bfloat16 [16, 2048, 768], P(('ctx', 'ep'), None, 'tp'), may hold values from -0.125 to 0.125
- expert_down: bfloat16 [16, 768, 2048], P(('ctx', 'ep'), 'tp'), may hold values from -0.21875 to 0.21875
Outputs:
- attended: bfloat16 [512, 2, 16, 128], P(('rep', 'ctx'), 'tp', 'ep'), parts along dimension 0
- mixture: bfloat16 [4096, 2048], P(('rep', 'ctx', 'ep'), 'tp'), parts along dimension 0
The draws below stay inside these ranges and needn't reach their ends.
There are 2 independent parts, one for each index of `rep`. The reference program is written for one: setup_inputs(seed, part) draws one part's arguments, and reference() takes and returns one part's arrays. A program takes and returns all parts, laid end to end along the dimension named above; an argument that names none is the same for every part. Nothing has to cross between parts.
Inputs may be any that keep to these rules, and one draw needn't show every extreme that they name: `routes`: within each aligned block of 128 rows (the rows of one device) no expert is named by more than 80 of them, a bound that some block reaches.
All inputs are finite; a program needn't handle non-finite values. Where the reference program divides by a largest or mean magnitude, that divisor is 1e-20 or more.
Results may differ from the reference program's by a relative error of at most 0.008.
Values may be sent and summed in bfloat16 or wider, within the bound.
No kernel may reach another device: no remote copies, remote signals or barrier semaphores. Data moves between devices by JAX's collectives and lax.ppermute only.
A program may use at most 128 MiB of HBM per device.

```python
import math
import jax
import jax.numpy as jnp
import numpy as np
from jax import lax

D = 2048
HID = 768
KVH = 2
GRP = 16
HD = 128
TOPK = 8
ROWS = 128
HS = 768
EXPERTS = 16
CAP = 80
TOKENS = 2048
QTOK = 256
KTOK = 512
N_TP = 1


def shared_keys(key):
    return jnp.clip(jax.random.normal(key, (KTOK, KVH, HD), jnp.float32), -6.0, 6.0)


def draw_key_rows(key, part):
    common = shared_keys(key)
    return jnp.clip(common, -6.5, 6.5).astype(jnp.bfloat16)


def draw_queries(key, part):
    key = jax.random.fold_in(key, 23)
    own_key = jax.random.fold_in(key, 0)
    result = 1.5 * jax.random.normal(own_key, (QTOK, KVH, GRP, HD), jnp.float32)
    return jnp.clip(result, -120.0, 120.0).astype(jnp.bfloat16)


def block_levels(key, dims, cuts, smallest, largest):
    def one(axis_at, blocks):
        draws = jax.random.uniform(jax.random.fold_in(jax.random.fold_in(key, 6), axis_at), (blocks,), jnp.float32, smallest / len(cuts), largest / len(cuts))
        return jnp.repeat(jnp.exp(draws), dims[axis_at] // blocks).reshape((-1,) + (1,) * (len(dims) - axis_at - 1))

    level = one(*cuts[0])
    for cut in cuts[1:]:
        level = level * one(*cut)
    return level


def deal_out(rng, own, number, rows, number_of, top, limit, lean):
    order = jax.random.permutation(rng, number_of)
    crowded, usual = portions_of(number_of, rows * top, limit, lean, True), portions_of(number_of, rows * top, limit, lean, False)
    places = jnp.arange(number_of)

    def named(sizes, rotation):
        used = int((sizes > 0).sum())
        fixed = max(1, used // 4)
        shifted = fixed + (places - fixed + rotation * (used - fixed)) % max(1, number_of - fixed)
        return jnp.zeros((number_of,), jnp.int32).at[order[jnp.where(places < fixed, places, shifted)]].set(jnp.asarray(sizes, jnp.int32))

    sizes = jnp.where(number % 4 == 0, named(crowded, number // 4), named(usual, number - number // 4 - 1))
    mixed = jax.random.permutation(jax.random.fold_in(own, 3), number_of)
    donor, taker = mixed[0:number_of // 2 * 2:2], mixed[1:number_of // 2 * 2:2]
    room = jnp.minimum(sizes[donor] - 1, limit - sizes[taker]) // 2
    room = jnp.where((donor == order[0]) | (taker == order[0]) | (sizes[taker] == 0), 0, jnp.maximum(room, 0))
    shifted = jax.random.randint(jax.random.fold_in(own, 4), (number_of // 2,), 0, 1 << 20) % (room + 1)
    sizes = sizes.at[donor].add(-shifted).at[taker].add(shifted)
    members = jnp.searchsorted(jnp.cumsum(sizes), jnp.arange(rows * top), side="right").astype(jnp.int32)
    table = members.reshape(top, rows).T
    table = table[jax.random.permutation(jax.random.fold_in(own, 1), rows)]
    rotation = jax.random.randint(jax.random.fold_in(own, 2), (rows, 1), 0, top)
    return jnp.take_along_axis(table, (jnp.arange(top)[None, :] + rotation) % top, axis=1)


def portions_of(number_of, total, most, slope, full):
    portions = [(1 << 20) // math.isqrt(grade ** slope) + 1 for grade in range(1, number_of + 1)]
    largest = most if full else min(most, max(-(-total // number_of), total * portions[0] // sum(portions)))
    least = 1 if total - largest >= number_of - 1 else 0
    counts, rest = [largest] + [least] * (number_of - 1), total - largest - least * (number_of - 1)
    while rest > 0:
        movable = [i for i in range(1, number_of) if counts[i] < largest] or [i for i in range(1, number_of) if counts[i] < most]
        pool, left = sum([portions[i] for i in movable]), rest
        for i in movable:
            extra = min(most - counts[i], max(1, left * portions[i] // pool), rest)
            counts[i] = counts[i] + extra
            rest = rest - extra
    return np.array(counts)


def gaussian(key, extent, scale, most, cuts=(), kind=jnp.bfloat16):
    drawn = jax.random.normal(key, extent, jnp.float32) * scale
    if len(cuts) > 0:
        drawn = block_levels(key, extent, cuts, -0.22, 0.18) * drawn
    return jnp.clip(drawn, min=-most, max=most).astype(kind)


def setup_inputs(seed: int = 0, part: int = 0) -> dict:
    key_list = jax.random.split(jax.random.key(seed), 10)
    part_keys = jax.random.split(jax.random.fold_in(key_list[9], part), 10)
    queries = draw_queries(jax.random.fold_in(jax.random.fold_in(key_list[9], part), 71), part)
    key_rows = draw_key_rows(jax.random.fold_in(jax.random.fold_in(key_list[9], part), 71), part)
    values = gaussian(part_keys[2], (KTOK, KVH, HD), 8.0, 48.0, ((0, 4),))
    offset = jax.random.randint(part_keys[3], (1,), 0, KTOK - QTOK + 1).astype(jnp.int32)
    tokens = gaussian(part_keys[4], (TOKENS, D), 1.0, 6.0, ((0, 16),))
    routes_keys = jax.random.split(jax.random.fold_in(part_keys[5], 1), TOKENS // ROWS)
    routes_turns = jax.random.permutation(jax.random.fold_in(part_keys[5], 3), TOKENS // ROWS)
    routes = jax.vmap(lambda own, number: deal_out(jax.random.fold_in(part_keys[5], 2), own, number, ROWS, EXPERTS, TOPK, CAP, 1))(routes_keys, routes_turns).reshape((TOKENS, TOPK))
    gate_share = jnp.clip(0.1 + 0.9 * jax.random.uniform(part_keys[6], (TOKENS, TOPK), jnp.float32) ** block_levels(part_keys[6], (TOKENS, TOPK), ((0, 16),), -0.2, 0.2), 0.1, 1.0)
    expert_gate = gaussian(key_list[7], (EXPERTS, D, HID), D ** -0.5, 0.125, ((0, 16),))
    expert_down = gaussian(key_list[8], (EXPERTS, HID, D), HID ** -0.5, 0.21875, ((0, 16),))
    return {"queries": queries, "key_rows": key_rows, "values": values, "offset": offset, "tokens": tokens, "routes": routes, "gate_share": gate_share, "expert_gate": expert_gate, "expert_down": expert_down}


def attend_block(query_block, query_pos, key_rows, values):
    inv_root = 1.0 / math.sqrt(HD)
    scores = jnp.einsum('qhgd,khd->qhgk', query_block.astype(jnp.float32), key_rows.astype(jnp.float32)) * inv_root
    key_pos = jnp.arange(KTOK, dtype=jnp.int32)
    visible = (key_pos[None, :] <= query_pos[:, None])[:, None, None, :]
    masked = jnp.where(visible, scores, -1e+30)
    highest = lax.optimization_barrier(jnp.max(masked, axis=-1, keepdims=True))
    weights = jnp.where(visible, jnp.exp(masked - highest), 0.0)
    row_total = lax.optimization_barrier(jnp.sum(weights, axis=-1))
    probs = weights.astype(jnp.bfloat16)
    mixed = jnp.einsum('qhgk,khd->qhgd', probs.astype(jnp.float32), values.astype(jnp.float32))
    return (mixed / row_total[..., None]).astype(jnp.bfloat16)

def reference(queries, key_rows, values, offset, tokens, routes, gate_share, expert_gate, expert_down):
    span_rows = math.gcd(QTOK, 256)
    positions = offset[0] + jnp.arange(QTOK, dtype=jnp.int32)

    def attend_inputs(inputs):
        return attend_block(inputs[0], inputs[1], key_rows, values)
    attended = lax.map(attend_inputs, (queries.reshape(QTOK // span_rows, span_rows, KVH, GRP, HD), positions.reshape(QTOK // span_rows, span_rows)))
    attended = attended.reshape(QTOK, KVH, GRP, HD)
    grouped = tokens.astype(jnp.float32).reshape(TOKENS, D // 128, 128)
    block_scale = (lax.optimization_barrier(jnp.max(jnp.abs(grouped), axis=-1)) + 1e-06).astype(jnp.bfloat16)
    coded_rows = (grouped / block_scale.astype(jnp.float32)[..., None]).astype(jnp.bfloat16)
    restored = (coded_rows.astype(jnp.float32) * block_scale.astype(jnp.float32)[..., None]).astype(jnp.bfloat16).reshape(TOKENS, D)
    shares = gate_share / lax.optimization_barrier(jnp.sum(gate_share, axis=1, keepdims=True))
    blocks_count = TOKENS // ROWS
    chosen = routes.reshape(blocks_count, ROWS * TOPK)
    onehot = (chosen[..., None] == jnp.arange(EXPERTS, dtype=jnp.int32)).astype(jnp.int32)
    earlier = jnp.cumsum(onehot, axis=1) - onehot
    slot_index = lax.optimization_barrier(jnp.sum(earlier * onehot, axis=-1))
    block_id = jnp.arange(blocks_count, dtype=jnp.int32)[:, None]
    target = (chosen * (blocks_count * CAP) + block_id * CAP + slot_index).reshape(-1).astype(jnp.int32)
    owners = jnp.repeat(jnp.arange(TOKENS, dtype=jnp.int32), TOPK)
    source = jnp.zeros((EXPERTS * blocks_count * CAP,), jnp.int32).at[target].set(owners).reshape(EXPERTS, blocks_count * CAP)
    weight = jnp.zeros((EXPERTS * blocks_count * CAP,), jnp.float32).at[target].set(shares.reshape(-1)).reshape(EXPERTS, blocks_count * CAP)

    def one_expert(running, inputs):
        row_ids, row_weights, gate_matrix, down_matrix = inputs
        picked = restored[row_ids]
        hidden = jax.nn.silu(jnp.dot(picked, gate_matrix, preferred_element_type=jnp.float32)).astype(jnp.bfloat16)
        summed = jnp.zeros((row_ids.shape[0], D), jnp.float32)
        for group_index in range(N_TP):
            group_out = jnp.dot(hidden[:, group_index * HS:(group_index + 1) * HS], down_matrix[group_index * HS:(group_index + 1) * HS], preferred_element_type=jnp.float32).astype(jnp.bfloat16)
            summed = summed + group_out.astype(jnp.float32)
        expert_out = summed.astype(jnp.bfloat16).astype(jnp.float32)
        return (running.at[row_ids].add(row_weights[:, None] * expert_out), None)
    mixture, unused = lax.scan(one_expert, jnp.zeros((TOKENS, D), jnp.float32), (source, weight, expert_gate, expert_down))
    return (attended, mixture.astype(jnp.bfloat16))
```

```python
import functools
import math

import jax
import jax.numpy as jnp
from jax import lax
from jax.experimental import pallas as pl
from jax.experimental.pallas import tpu as pltpu
from jax.sharding import PartitionSpec as P

TAG = 128


def attention_shard(queries, key_rows, values, offset):
    query_rows, head_count, group_count, head_size = queries.shape
    inv_root = 1.0 / math.sqrt(head_size)
    query_pos = (
        offset[0] + lax.axis_index("ctx") * query_rows + jnp.arange(query_rows, dtype=jnp.int32)
    )
    row_pos = jnp.tile(query_pos, group_count)
    head_rows = jnp.transpose(queries, (1, 2, 0, 3)).reshape(
        head_count, group_count * query_rows, head_size
    )
    state_shape = (head_count, group_count * query_rows)
    highest = jnp.full(state_shape, -1e30, jnp.float32)
    key_piece = lax.all_gather(key_rows, "ctx", axis=0, tiled=True)
    value_piece = lax.all_gather(values, "ctx", axis=0, tiled=True)
    scores = (
        jnp.einsum("hrd,khd->hrk", head_rows, key_piece, preferred_element_type=jnp.float32)
        * inv_root
    )
    key_pos = jnp.arange(key_piece.shape[0], dtype=jnp.int32)
    visible = (key_pos[None, :] <= row_pos[:, None])[None]
    masked = jnp.where(visible, scores, -1e30)
    newest = jnp.maximum(highest, jnp.max(masked, axis=-1))
    weights = jnp.where(visible, jnp.exp(masked - newest[..., None]), 0.0)
    running = jnp.sum(weights, axis=-1)
    summed = jnp.einsum(
        "hrk,khd->hrd",
        weights.astype(jnp.bfloat16),
        value_piece,
        preferred_element_type=jnp.float32,
    )
    highest, running, summed = (newest, running, summed)
    result = (summed / running[..., None]).astype(jnp.bfloat16)
    return jnp.transpose(
        result.reshape(head_count, group_count, query_rows, head_size), (2, 0, 1, 3)
    )


def expert_pass(arrived_rows, expert_gate, expert_down):
    coded_in, scale_in = arrived_rows
    senders, capacity, features = coded_in.shape
    resident = expert_gate.shape[0]
    restored = (
        coded_in.astype(jnp.float32).reshape(senders, capacity, scale_in.shape[2], -1)
        * scale_in.astype(jnp.float32)[..., None]
    ).astype(jnp.bfloat16)
    restored = restored.reshape(senders // resident, resident, capacity, features)
    hidden = jax.nn.silu(
        jnp.einsum("sfcd,fdh->sfch", restored, expert_gate, preferred_element_type=jnp.float32)
    ).astype(jnp.bfloat16)
    result = jnp.einsum(
        "sfch,fhd->sfcd", hidden, expert_down, preferred_element_type=jnp.float32
    ).astype(jnp.bfloat16)
    result = result.reshape(senders, capacity, features)
    return result


def body(queries, key_rows, values, offset, tokens, routes, gate_share, expert_gate, expert_down):
    attended = attention_shard(queries, key_rows, values, offset)
    rows_here, features = tokens.shape
    topk_count = routes.shape[1]
    resident = expert_gate.shape[0]
    ctx_devices = lax.axis_size("ctx")
    ep_devices = lax.axis_size("ep")
    expert_total = ctx_devices * ep_devices * resident
    capacity = min(rows_here, max(2, 5 * rows_here * topk_count // (4 * expert_total)))
    scale_blocks = features // 128
    grouped = tokens.astype(jnp.float32).reshape(rows_here, scale_blocks, 128)
    block_scale = (jnp.max(jnp.abs(grouped), axis=-1) + 1e-06).astype(jnp.bfloat16)
    coded_rows = (
        (grouped / block_scale.astype(jnp.float32)[..., None])
        .astype(jnp.bfloat16)
        .reshape(rows_here, features)
    )
    pair_count = rows_here * topk_count
    chosen = routes.reshape(pair_count)
    onehot = (chosen[:, None] == jnp.arange(expert_total, dtype=jnp.int32)[None, :]).astype(
        jnp.bfloat16
    )
    before_mask = (jnp.arange(pair_count)[:, None] > jnp.arange(pair_count)[None, :]).astype(
        jnp.bfloat16
    )
    earlier = jnp.dot(before_mask, onehot, preferred_element_type=jnp.float32)
    slot_index = jnp.sum(earlier * onehot.astype(jnp.float32), axis=1).astype(jnp.int32)
    target = chosen * capacity + slot_index
    matches = (
        jnp.arange(expert_total * capacity, dtype=jnp.int32)[:, None, None]
        == target.reshape(rows_here, topk_count)[None]
    )
    placing = jnp.sum(matches.astype(jnp.int32), axis=2).astype(jnp.bfloat16)
    outgoing = (
        jnp.dot(placing, coded_rows, preferred_element_type=jnp.float32)
        .astype(jnp.bfloat16)
        .reshape(expert_total, capacity, -1)
    )
    outgoing_scale = (
        jnp.dot(placing, block_scale, preferred_element_type=jnp.float32)
        .astype(jnp.bfloat16)
        .reshape(expert_total, capacity, -1)
    )
    computed = expert_pass(
        (
            lax.all_to_all(outgoing, ("ctx", "ep"), split_axis=0, concat_axis=0, tiled=True),
            lax.all_to_all(outgoing_scale, ("ctx", "ep"), split_axis=0, concat_axis=0, tiled=True),
        ),
        expert_gate,
        expert_down,
    )
    returned = lax.all_to_all(computed, ("ctx", "ep"), split_axis=0, concat_axis=0, tiled=True)
    back_width = returned.shape[-1]
    flat_back = returned.reshape(expert_total * capacity, back_width)
    picked = jnp.take(flat_back, target, axis=0)
    parts_in = lax.all_to_all(
        picked.reshape(pair_count, 1, back_width), "tp", split_axis=2, concat_axis=1, tiled=True
    )
    picked = jnp.sum(parts_in.astype(jnp.float32), axis=1).astype(jnp.bfloat16)
    picked = picked.reshape(rows_here, topk_count, -1)
    shares = gate_share / jnp.sum(gate_share, axis=1, keepdims=True)
    mixture = jnp.sum(shares[..., None] * picked.astype(jnp.float32), axis=1).astype(jnp.bfloat16)
    return (attended, mixture)


def prepare_kernel(tokens_ref, routes_ref, gate_ref, out_ref, *, expert_total):
    rows, features = tokens_ref.shape
    for block in range(features // 128):
        cols = slice(block * 128, (block + 1) * 128)
        part = tokens_ref[:, cols].astype(jnp.float32)
        scale = jnp.max(jnp.abs(part), axis=1, keepdims=True) + 1e-06
        scale = scale.astype(jnp.bfloat16).astype(jnp.float32)
        coded = (part / scale).astype(jnp.bfloat16).astype(jnp.float32)
        out_ref[:, cols] = (coded * scale).astype(jnp.bfloat16)
    gate = gate_ref[...]
    shares = gate / jnp.sum(gate, axis=1, keepdims=True)
    lane = lax.broadcasted_iota(jnp.int32, (rows, TAG), 1)
    expert = lax.rem(lane, expert_total)
    dense = jnp.zeros((rows, TAG), jnp.float32)
    for k in range(gate.shape[1]):
        dense += jnp.where(routes_ref[:, k : k + 1] == expert, shares[:, k : k + 1], 0.0)
    high = dense.astype(jnp.bfloat16).astype(jnp.float32)
    tag = jnp.where(lane < expert_total, high, jnp.where(lane < 2 * expert_total, dense - high, 0.0))
    out_ref[:, features:] = tag.astype(jnp.bfloat16)


def prepare(tokens, routes, gate_share, expert_total):
    rows, features = tokens.shape
    return pl.pallas_call(
        functools.partial(prepare_kernel, expert_total=expert_total),
        out_shape=jax.ShapeDtypeStruct((rows, features + TAG), jnp.bfloat16),
    )(tokens, routes, gate_share)


def experts_kernel(ids_ref, *refs, count, expert_total, up_steps, up_tile):
    blocks = refs[:count]
    gate_a, gate_b, down_a, down_b = refs[count : count + 4]
    outs = refs[count + 4 : 2 * count + 4]
    rows_in, shares_in, hidden = refs[2 * count + 4 :]
    step = pl.program_id(0)
    rows, width = blocks[0].shape
    features = width - TAG
    half = up_steps // 2

    @pl.when(step == 0)
    def _():
        lane = lax.broadcasted_iota(jnp.int32, (rows, TAG), 1)
        for i, block in enumerate(blocks):
            here = slice(i * rows, (i + 1) * rows)
            rows_in[here, :] = block[:, :features]
            tag = block[:, features:].astype(jnp.float32)
            for j in range(2):
                expert = ids_ref[j]
                mine = (lane == expert) | (lane == expert + expert_total)
                share = jnp.sum(jnp.where(mine, tag, 0.0), axis=1, keepdims=True)
                shares_in[j, here, :] = jnp.broadcast_to(share, (rows, TAG))

    def up(weights_ref, j, tile):
        value = jnp.dot(rows_in[...], weights_ref[...], preferred_element_type=jnp.float32)
        value = value / (1.0 + jnp.exp(-value)) * shares_in[j, :, :1]
        start = pl.multiple_of((j * half + tile) * up_tile, up_tile)
        hidden[:, pl.ds(start, up_tile)] = value.astype(jnp.bfloat16)

    @pl.when(step < half)
    def _():
        up(gate_a, 0, step)

    @pl.when((step >= half) & (step < up_steps))
    def _():
        up(gate_b, 1, step - half)

    @pl.when(step >= up_steps)
    def _():
        units = half * up_tile
        total = jnp.dot(hidden[:, :units], down_a[...], preferred_element_type=jnp.float32)
        total += jnp.dot(hidden[:, units:], down_b[...], preferred_element_type=jnp.float32)
        for i, out in enumerate(outs):
            out[...] = total[i * rows : (i + 1) * rows].astype(jnp.bfloat16)


def experts(ids, blocks, gate_a, gate_b, down_a, down_b, expert_total):
    count = len(blocks)
    rows, width = blocks[0].shape
    features, units = gate_a.shape
    up_tile, down_tile = 256, 512
    half = units // up_tile
    up_steps = 2 * half
    down_steps = features // down_tile
    whole = pl.BlockSpec((rows, width), lambda i: (0, 0))
    down_spec = pl.BlockSpec((units, down_tile), lambda i: (0, jnp.maximum(i - up_steps, 0)))
    out_spec = pl.BlockSpec((rows, down_tile), lambda i: (0, jnp.maximum(i - up_steps, 0)))
    flops = 2 * 2 * 2 * count * rows * features * units
    return pl.pallas_call(
        functools.partial(
            experts_kernel,
            count=count,
            expert_total=expert_total,
            up_steps=up_steps,
            up_tile=up_tile,
        ),
        grid=(up_steps + down_steps,),
        in_specs=[pl.BlockSpec(memory_space=pltpu.SMEM)]
        + [whole] * count
        + [
            pl.BlockSpec((features, up_tile), lambda i: (0, jnp.minimum(i, half - 1))),
            pl.BlockSpec((features, up_tile), lambda i: (0, jnp.clip(i - half, 0, half - 1))),
            down_spec,
            down_spec,
        ],
        out_specs=[out_spec] * count,
        out_shape=[jax.ShapeDtypeStruct((rows, features), jnp.bfloat16)] * count,
        scratch_shapes=[
            pltpu.VMEM((count * rows, features), jnp.bfloat16),
            pltpu.VMEM((2, count * rows, TAG), jnp.float32),
            pltpu.VMEM((count * rows, 2 * units), jnp.bfloat16),
        ],
        compiler_params=pltpu.CompilerParams(
            dimension_semantics=("arbitrary",), vmem_limit_bytes=48 * 1024 * 1024
        ),
        cost_estimate=pl.CostEstimate(
            flops=flops, bytes_accessed=8 * features * units, transcendentals=0
        ),
    )(ids, *blocks, gate_a, gate_b, down_a, down_b)


NEAR = [(0, 1), (1, 0), (2, 3), (3, 2)]
MIDDLE = [(1, 2), (2, 1)]
OUTWARD = [(1, 0), (2, 3)]
INWARD = [(0, 1), (3, 2)]
ACROSS = [(i, i ^ 2) for i in range(4)]
SIBLING = [(i, i ^ 1) for i in range(4)]


def along_z(array, pairs):
    return lax.ppermute(array, "ctx", pairs)


def across(array):
    return lax.ppermute(array, "ep", ACROSS)


def added(*terms):
    return sum(term.astype(jnp.float32) for term in terms).astype(jnp.bfloat16)


def attention_pieces(queries, key_rows, values, offset):
    query_rows, head_count, group_count, head_size = queries.shape
    here = lax.axis_index("ctx")
    span = key_rows.shape[0]
    both = jnp.concatenate(
        [key_rows.reshape(span, -1), values.reshape(span, -1)], axis=1
    )
    pieces = [both] + [
        lax.ppermute(both, "ctx", [(i, i ^ j) for i in range(4)]) for j in (1, 2, 3)
    ]
    pieces = jnp.concatenate(pieces, axis=0)
    total = pieces.shape[0]
    key_piece = pieces[:, : head_count * head_size].reshape(total, head_count, head_size)
    value_piece = pieces[:, head_count * head_size :].reshape(total, head_count, head_size)
    key_pos = jnp.arange(total, dtype=jnp.int32)
    key_pos = jnp.bitwise_xor(key_pos // span, here) * span + key_pos % span
    query_pos = offset[0] + here * query_rows + jnp.arange(query_rows, dtype=jnp.int32)
    row_pos = jnp.tile(query_pos, group_count)
    head_rows = jnp.transpose(queries, (1, 2, 0, 3)).reshape(
        head_count, group_count * query_rows, head_size
    )
    scores = jnp.einsum(
        "hrd,khd->hrk", head_rows, key_piece, preferred_element_type=jnp.float32
    ) * (1.0 / math.sqrt(head_size))
    visible = (key_pos[None, :] <= row_pos[:, None])[None]
    masked = jnp.where(visible, scores, -1e30)
    newest = jnp.max(masked, axis=-1, keepdims=True)
    weights = jnp.where(visible, jnp.exp(masked - newest), 0.0)
    running = jnp.sum(weights, axis=-1, keepdims=True)
    summed = jnp.einsum(
        "hrk,khd->hrd",
        weights.astype(jnp.bfloat16),
        value_piece,
        preferred_element_type=jnp.float32,
    )
    result = (summed / running).astype(jnp.bfloat16)
    return jnp.transpose(
        result.reshape(head_count, group_count, query_rows, head_size), (2, 0, 1, 3)
    )


def plane_body(queries, key_rows, values, offset, tokens, routes, gate_share, expert_gate, expert_down):
    expert_total = lax.axis_size("ctx") * lax.axis_size("ep")
    z = lax.axis_index("ctx")
    middle = (z == 1) | (z == 2)
    own_expert = z * lax.axis_size("ep") + lax.axis_index("ep")
    ids = jnp.stack([own_expert, own_expert ^ 1]).astype(jnp.int32)
    gate_a, down_a = expert_gate[0], expert_down[0]
    own = prepare(tokens, routes, gate_share, expert_total)
    near = along_z(own, NEAR)
    mid_one = along_z(own, MIDDLE)
    own_x = across(own)
    gate_b = lax.ppermute(gate_a, "ep", SIBLING)
    down_b = lax.ppermute(down_a, "ep", SIBLING)

    def run(*blocks):
        return experts(ids, blocks, gate_a, gate_b, down_a, down_b, expert_total)

    mid_two = along_z(near, MIDDLE)
    end_one = along_z(mid_one, OUTWARD)
    near_x = across(near)
    attended = attention_pieces(queries, key_rows, values, offset)
    part_own, part_own_x, part_near = run(own, own_x, near)
    end_two = along_z(mid_two, OUTWARD)
    second = jnp.where(middle, mid_one, end_one)
    second_x = across(second)
    part_near_x, part_second = run(near_x, second)
    third = jnp.where(middle, mid_two, end_two)
    third_x = across(third)
    part_second_x, part_third = run(second_x, third)
    (part_third_x,) = run(third_x)

    sum_third = added(part_third, across(part_third_x))
    back_two = along_z(sum_third, INWARD)
    sum_second = added(part_second, across(part_second_x))
    back_mid_two = along_z(added(sum_third, back_two), MIDDLE)
    back_one = along_z(sum_second, INWARD)
    sum_near = added(part_near, across(part_near_x), back_mid_two)
    back_mid_one = along_z(added(sum_second, back_one), MIDDLE)
    back_near = along_z(sum_near, NEAR)
    mixture = added(part_own, across(part_own_x), back_mid_one, back_near)
    return (attended, mixture)


def solution(mesh):
    plane = dict(mesh.shape)
    plane = plane["ctx"] == 4 and plane["ep"] == 4 and plane["tp"] == 1
    return jax.shard_map(
        plane_body if plane else body,
        mesh=mesh,
        in_specs=(
            P(("rep", "ctx"), "tp", "ep", None),
            P(("rep", "ctx"), "tp", None),
            P(("rep", "ctx"), "tp", None),
            P("rep"),
            P(("rep", "ctx", "ep"), None),
            P(("rep", "ctx", "ep"), None),
            P(("rep", "ctx", "ep"), None),
            P(("ctx", "ep"), None, "tp"),
            P(("ctx", "ep"), "tp", None),
        ),
        out_specs=(P(("rep", "ctx"), "tp", "ep", None), P(("rep", "ctx", "ep"), "tp")),
        check_vma=False,
    )
```

```python
import functools
import math

import jax
import jax.numpy as jnp
from jax import lax
from jax.experimental import pallas as pl
from jax.experimental.pallas import tpu as pltpu
from jax.sharding import PartitionSpec as P

TAG = 128


def attention_shard(queries, key_rows, values, offset):
    query_rows, head_count, group_count, head_size = queries.shape
    inv_root = 1.0 / math.sqrt(head_size)
    query_pos = (
        offset[0] + lax.axis_index("ctx") * query_rows + jnp.arange(query_rows, dtype=jnp.int32)
    )
    row_pos = jnp.tile(query_pos, group_count)
    head_rows = jnp.transpose(queries, (1, 2, 0, 3)).reshape(
        head_count, group_count * query_rows, head_size
    )
    state_shape = (head_count, group_count * query_rows)
    highest = jnp.full(state_shape, -1e30, jnp.float32)
    key_piece = lax.all_gather(key_rows, "ctx", axis=0, tiled=True)
    value_piece = lax.all_gather(values, "ctx", axis=0, tiled=True)
    scores = (
        jnp.einsum("hrd,khd->hrk", head_rows, key_piece, preferred_element_type=jnp.float32)
        * inv_root
    )
    key_pos = jnp.arange(key_piece.shape[0], dtype=jnp.int32)
    visible = (key_pos[None, :] <= row_pos[:, None])[None]
    masked = jnp.where(visible, scores, -1e30)
    newest = jnp.maximum(highest, jnp.max(masked, axis=-1))
    weights = jnp.where(visible, jnp.exp(masked - newest[..., None]), 0.0)
    running = jnp.sum(weights, axis=-1)
    summed = jnp.einsum(
        "hrk,khd->hrd",
        weights.astype(jnp.bfloat16),
        value_piece,
        preferred_element_type=jnp.float32,
    )
    highest, running, summed = (newest, running, summed)
    result = (summed / running[..., None]).astype(jnp.bfloat16)
    return jnp.transpose(
        result.reshape(head_count, group_count, query_rows, head_size), (2, 0, 1, 3)
    )


def expert_pass(arrived_rows, expert_gate, expert_down):
    coded_in, scale_in = arrived_rows
    senders, capacity, features = coded_in.shape
    resident = expert_gate.shape[0]
    restored = (
        coded_in.astype(jnp.float32).reshape(senders, capacity, scale_in.shape[2], -1)
        * scale_in.astype(jnp.float32)[..., None]
    ).astype(jnp.bfloat16)
    restored = restored.reshape(senders // resident, resident, capacity, features)
    hidden = jax.nn.silu(
        jnp.einsum("sfcd,fdh->sfch", restored, expert_gate, preferred_element_type=jnp.float32)
    ).astype(jnp.bfloat16)
    result = jnp.einsum(
        "sfch,fhd->sfcd", hidden, expert_down, preferred_element_type=jnp.float32
    ).astype(jnp.bfloat16)
    result = result.reshape(senders, capacity, features)
    return result


def body(queries, key_rows, values, offset, tokens, routes, gate_share, expert_gate, expert_down):
    attended = attention_shard(queries, key_rows, values, offset)
    rows_here, features = tokens.shape
    topk_count = routes.shape[1]
    resident = expert_gate.shape[0]
    ctx_devices = lax.axis_size("ctx")
    ep_devices = lax.axis_size("ep")
    expert_total = ctx_devices * ep_devices * resident
    capacity = min(rows_here, max(2, 5 * rows_here * topk_count // (4 * expert_total)))
    scale_blocks = features // 128
    grouped = tokens.astype(jnp.float32).reshape(rows_here, scale_blocks, 128)
    block_scale = (jnp.max(jnp.abs(grouped), axis=-1) + 1e-06).astype(jnp.bfloat16)
    coded_rows = (
        (grouped / block_scale.astype(jnp.float32)[..., None])
        .astype(jnp.bfloat16)
        .reshape(rows_here, features)
    )
    pair_count = rows_here * topk_count
    chosen = routes.reshape(pair_count)
    onehot = (chosen[:, None] == jnp.arange(expert_total, dtype=jnp.int32)[None, :]).astype(
        jnp.bfloat16
    )
    before_mask = (jnp.arange(pair_count)[:, None] > jnp.arange(pair_count)[None, :]).astype(
        jnp.bfloat16
    )
    earlier = jnp.dot(before_mask, onehot, preferred_element_type=jnp.float32)
    slot_index = jnp.sum(earlier * onehot.astype(jnp.float32), axis=1).astype(jnp.int32)
    target = chosen * capacity + slot_index
    matches = (
        jnp.arange(expert_total * capacity, dtype=jnp.int32)[:, None, None]
        == target.reshape(rows_here, topk_count)[None]
    )
    placing = jnp.sum(matches.astype(jnp.int32), axis=2).astype(jnp.bfloat16)
    outgoing = (
        jnp.dot(placing, coded_rows, preferred_element_type=jnp.float32)
        .astype(jnp.bfloat16)
        .reshape(expert_total, capacity, -1)
    )
    outgoing_scale = (
        jnp.dot(placing, block_scale, preferred_element_type=jnp.float32)
        .astype(jnp.bfloat16)
        .reshape(expert_total, capacity, -1)
    )
    computed = expert_pass(
        (
            lax.all_to_all(outgoing, ("ctx", "ep"), split_axis=0, concat_axis=0, tiled=True),
            lax.all_to_all(outgoing_scale, ("ctx", "ep"), split_axis=0, concat_axis=0, tiled=True),
        ),
        expert_gate,
        expert_down,
    )
    returned = lax.all_to_all(computed, ("ctx", "ep"), split_axis=0, concat_axis=0, tiled=True)
    back_width = returned.shape[-1]
    flat_back = returned.reshape(expert_total * capacity, back_width)
    picked = jnp.take(flat_back, target, axis=0)
    parts_in = lax.all_to_all(
        picked.reshape(pair_count, 1, back_width), "tp", split_axis=2, concat_axis=1, tiled=True
    )
    picked = jnp.sum(parts_in.astype(jnp.float32), axis=1).astype(jnp.bfloat16)
    picked = picked.reshape(rows_here, topk_count, -1)
    shares = gate_share / jnp.sum(gate_share, axis=1, keepdims=True)
    mixture = jnp.sum(shares[..., None] * picked.astype(jnp.float32), axis=1).astype(jnp.bfloat16)
    return (attended, mixture)


def prepare_kernel(tokens_ref, routes_ref, gate_ref, out_ref, *, expert_total):
    rows, features = tokens_ref.shape
    gate = gate_ref[...]
    shares = gate / jnp.sum(gate, axis=0, keepdims=True)
    line = lax.broadcasted_iota(jnp.int32, (TAG, rows), 0)
    expert = lax.rem(line, expert_total)
    dense = jnp.zeros((TAG, rows), jnp.float32)
    for k in range(gate.shape[0]):
        dense += jnp.where(routes_ref[k : k + 1, :] == expert, shares[k : k + 1, :], 0.0)
    high = dense.astype(jnp.bfloat16).astype(jnp.float32)
    tag = jnp.where(line < expert_total, high, jnp.where(line < 2 * expert_total, dense - high, 0.0))
    out_ref[:, features:] = tag.T.astype(jnp.bfloat16)
    for block in range(features // 128):
        cols = slice(block * 128, (block + 1) * 128)
        part = tokens_ref[:, cols].astype(jnp.float32)
        scale = jnp.max(jnp.abs(part), axis=1, keepdims=True) + 1e-06
        scale = scale.astype(jnp.bfloat16).astype(jnp.float32)
        coded = (part / scale).astype(jnp.bfloat16).astype(jnp.float32)
        out_ref[:, cols] = (coded * scale).astype(jnp.bfloat16)


def prepare(tokens, routes, gate_share, expert_total):
    rows, features = tokens.shape
    return pl.pallas_call(
        functools.partial(prepare_kernel, expert_total=expert_total),
        out_shape=jax.ShapeDtypeStruct((rows, features + TAG), jnp.bfloat16),
    )(tokens, routes.T, gate_share.T)


def experts_kernel(ids_ref, *refs, count, expert_total):
    blocks = refs[:count]
    gates, downs = refs[count : count + 2], refs[count + 2 : count + 4]
    outs = refs[count + 4 : 2 * count + 4]
    rows_in, shares_in, hidden = refs[2 * count + 4 :]
    rows, width = blocks[0].shape
    features = width - TAG
    units = gates[0].shape[1]
    up_tile, down_tile = 256, 512
    lane = lax.broadcasted_iota(jnp.int32, (rows, TAG), 1)
    for i, block in enumerate(blocks):
        here = slice(i * rows, (i + 1) * rows)
        rows_in[here, :] = block[:, :features]
        tag = block[:, features:].astype(jnp.float32)
        for j in range(2):
            mine = (lane == ids_ref[j]) | (lane == ids_ref[j] + expert_total)
            share = jnp.sum(jnp.where(mine, tag, 0.0), axis=1, keepdims=True)
            shares_in[j, here, :] = jnp.broadcast_to(share, (rows, TAG))
    for j in range(2):
        for start in range(0, units, up_tile):
            value = jnp.dot(
                rows_in[...],
                gates[j][:, start : start + up_tile],
                preferred_element_type=jnp.float32,
            )
            value = value / (1.0 + jnp.exp(-value)) * shares_in[j, :, :1]
            first = j * units + start
            hidden[:, first : first + up_tile] = value.astype(jnp.bfloat16)
    for start in range(0, features, down_tile):
        cols = slice(start, start + down_tile)
        total = jnp.dot(hidden[:, :units], downs[0][:, cols], preferred_element_type=jnp.float32)
        total += jnp.dot(hidden[:, units:], downs[1][:, cols], preferred_element_type=jnp.float32)
        for i, out in enumerate(outs):
            out[:, cols] = total[i * rows : (i + 1) * rows].astype(jnp.bfloat16)


def experts(ids, blocks, gate_a, gate_b, down_a, down_b, expert_total):
    count = len(blocks)
    rows, width = blocks[0].shape
    features, units = gate_a.shape
    inside = pl.BlockSpec(memory_space=pltpu.VMEM)
    return pl.pallas_call(
        functools.partial(experts_kernel, count=count, expert_total=expert_total),
        in_specs=[pl.BlockSpec(memory_space=pltpu.SMEM)] + [inside] * (count + 4),
        out_specs=[inside] * count,
        out_shape=[jax.ShapeDtypeStruct((rows, features), jnp.bfloat16)] * count,
        scratch_shapes=[
            pltpu.VMEM((count * rows, features), jnp.bfloat16),
            pltpu.VMEM((2, count * rows, TAG), jnp.float32),
            pltpu.VMEM((count * rows, 2 * units), jnp.bfloat16),
        ],
        compiler_params=pltpu.CompilerParams(vmem_limit_bytes=16 * 1024 * 1024),
        cost_estimate=pl.CostEstimate(
            flops=8 * count * rows * features * units,
            bytes_accessed=8 * features * units,
            transcendentals=0,
        ),
    )(ids, *blocks, gate_a, gate_b, down_a, down_b)


def attention_kernel(where_ref, queries_ref, *refs, heads, head_size):
    pieces, out_ref = refs[:-1], refs[-1]
    query_rows, width = queries_ref.shape
    groups = width // (heads * head_size)
    span = pieces[0].shape[0]
    row = lax.broadcasted_iota(jnp.int32, (query_rows, span), 0)
    col = lax.broadcasted_iota(jnp.int32, (query_rows, span), 1)
    seen = [
        jnp.concatenate([where_ref[p] + col <= where_ref[len(pieces)] + row] * groups, axis=0)
        for p in range(len(pieces))
    ]
    for h in range(heads):
        first = h * groups * head_size
        rows = jnp.concatenate(
            [
                queries_ref[:, first + g * head_size : first + (g + 1) * head_size]
                for g in range(groups)
            ],
            axis=0,
        )
        scores = []
        for p, piece in enumerate(pieces):
            keys = piece[:, h * head_size : (h + 1) * head_size]
            value = lax.dot_general(
                rows, keys, (((1,), (1,)), ((), ())), preferred_element_type=jnp.float32
            ) * (1.0 / math.sqrt(head_size))
            scores.append(jnp.where(seen[p], value, -1e30))
        top = scores[0].max(axis=1, keepdims=True)
        for value in scores[1:]:
            top = jnp.maximum(top, value.max(axis=1, keepdims=True))
        running = jnp.zeros_like(top)
        summed = jnp.zeros((rows.shape[0], head_size), jnp.float32)
        for p, piece in enumerate(pieces):
            weights = jnp.where(seen[p], jnp.exp(scores[p] - top), 0.0)
            running += weights.sum(axis=1, keepdims=True)
            content = piece[:, (heads + h) * head_size : (heads + h + 1) * head_size]
            summed += jnp.dot(
                weights.astype(jnp.bfloat16), content, preferred_element_type=jnp.float32
            )
        result = (summed / running).astype(jnp.bfloat16)
        for g in range(groups):
            out_ref[:, first + g * head_size : first + (g + 1) * head_size] = result[
                g * query_rows : (g + 1) * query_rows
            ]


def attention_pieces(queries, pieces, positions, heads, head_size):
    query_rows, width = queries.shape
    inside = pl.BlockSpec(memory_space=pltpu.VMEM)
    return pl.pallas_call(
        functools.partial(attention_kernel, heads=heads, head_size=head_size),
        in_specs=[pl.BlockSpec(memory_space=pltpu.SMEM)] + [inside] * (1 + len(pieces)),
        out_specs=inside,
        out_shape=jax.ShapeDtypeStruct((query_rows, width), jnp.bfloat16),
        cost_estimate=pl.CostEstimate(
            flops=10**9, bytes_accessed=4 * 10**6, transcendentals=0
        ),
    )(positions, queries, *pieces)


NEAR = [(0, 1), (1, 0), (2, 3), (3, 2)]
MIDDLE = [(1, 2), (2, 1)]
OUTWARD = [(1, 0), (2, 3)]
INWARD = [(0, 1), (3, 2)]
ACROSS = [(i, i ^ 2) for i in range(4)]
SIBLING = [(i, i ^ 1) for i in range(4)]


def along_z(array, pairs):
    return lax.ppermute(array, "ctx", pairs)


def across(array):
    return lax.ppermute(array, "ep", ACROSS)


def added(*terms):
    return sum(term.astype(jnp.float32) for term in terms).astype(jnp.bfloat16)


def together(*arrays):
    return lax.optimization_barrier(arrays)


def plane_body(queries, key_rows, values, offset, tokens, routes, gate_share, expert_gate, expert_down):
    expert_total = lax.axis_size("ctx") * lax.axis_size("ep")
    z = lax.axis_index("ctx")
    middle = (z == 1) | (z == 2)
    own_expert = z * lax.axis_size("ep") + lax.axis_index("ep")
    ids = jnp.stack([own_expert, own_expert ^ 1]).astype(jnp.int32)
    span, heads, head_size = key_rows.shape
    query_rows = queries.shape[0]
    places = [z, z ^ 1, z ^ 2, z ^ 3]
    positions = jnp.stack([p * span for p in places] + [offset[0] + z * query_rows])
    gate_a, down_a = expert_gate[0], expert_down[0]
    gate_b = lax.ppermute(gate_a, "ep", SIBLING)
    down_b = lax.ppermute(down_a, "ep", SIBLING)

    def run(*blocks):
        return experts(ids, blocks, gate_a, gate_b, down_a, down_b, expert_total)

    own = prepare(tokens, routes, gate_share, expert_total)
    own_x = across(own)
    near = along_z(own, NEAR)
    mid_one = along_z(own, MIDDLE)
    near, mid_one, own_x, gate_b, down_b = together(near, mid_one, own_x, gate_b, down_b)

    near_x = across(near)
    mid_two = along_z(near, MIDDLE)
    end_one = along_z(mid_one, OUTWARD)
    part_own, part_own_x, part_near = run(own, own_x, near)
    second = jnp.where(middle, mid_one, end_one)
    second, mid_two, near_x, part_own, part_own_x, part_near = together(
        second, mid_two, near_x, part_own, part_own_x, part_near
    )

    second_x = across(second)
    end_two = along_z(mid_two, OUTWARD)
    part_near_x, part_second = run(near_x, second)
    third = jnp.where(middle, mid_two, end_two)
    keys = jnp.concatenate([key_rows.reshape(span, -1), values.reshape(span, -1)], axis=1)
    flat = queries.reshape(query_rows, -1)
    third, second_x, part_near_x, part_second, keys, flat = together(
        third, second_x, part_near_x, part_second, keys, flat
    )

    third_x = across(third)
    pieces = [keys] + [along_z(keys, [(i, i ^ j) for i in range(4)]) for j in (1, 2, 3)]
    part_second_x, part_third = run(second_x, third)
    third_x, part_second_x, part_third, *pieces = together(
        third_x, part_second_x, part_third, *pieces
    )
    (part_third_x,) = run(third_x)

    back_third = across(part_third_x)
    attended = attention_pieces(flat, pieces, positions, heads, head_size).reshape(queries.shape)
    back_third, attended = together(back_third, attended)
    sum_third = added(part_third, back_third)
    back_two = along_z(sum_third, INWARD)
    sum_second = added(part_second, across(part_second_x))
    back_mid_two = along_z(added(sum_third, back_two), MIDDLE)
    back_one = along_z(sum_second, INWARD)
    sum_near = added(part_near, across(part_near_x), back_mid_two)
    back_mid_one = along_z(added(sum_second, back_one), MIDDLE)
    back_near = along_z(sum_near, NEAR)
    mixture = added(part_own, across(part_own_x), back_mid_one, back_near)
    return (attended, mixture)


def solution(mesh):
    plane = dict(mesh.shape)
    plane = plane["ctx"] == 4 and plane["ep"] == 4 and plane["tp"] == 1
    return jax.shard_map(
        plane_body if plane else body,
        mesh=mesh,
        in_specs=(
            P(("rep", "ctx"), "tp", "ep", None),
            P(("rep", "ctx"), "tp", None),
            P(("rep", "ctx"), "tp", None),
            P("rep"),
            P(("rep", "ctx", "ep"), None),
            P(("rep", "ctx", "ep"), None),
            P(("rep", "ctx", "ep"), None),
            P(("ctx", "ep"), None, "tp"),
            P(("ctx", "ep"), "tp", None),
        ),
        out_specs=(P(("rep", "ctx"), "tp", "ep", None), P(("rep", "ctx", "ep"), "tp")),
        check_vma=False,
    )
```

```python
import functools
import math

import jax
import jax.numpy as jnp
from jax import lax
from jax.experimental import pallas as pl
from jax.experimental.pallas import tpu as pltpu
from jax.sharding import PartitionSpec as P

TAG = 128


def attention_shard(queries, key_rows, values, offset):
    query_rows, head_count, group_count, head_size = queries.shape
    inv_root = 1.0 / math.sqrt(head_size)
    query_pos = (
        offset[0] + lax.axis_index("ctx") * query_rows + jnp.arange(query_rows, dtype=jnp.int32)
    )
    row_pos = jnp.tile(query_pos, group_count)
    head_rows = jnp.transpose(queries, (1, 2, 0, 3)).reshape(
        head_count, group_count * query_rows, head_size
    )
    state_shape = (head_count, group_count * query_rows)
    highest = jnp.full(state_shape, -1e30, jnp.float32)
    key_piece = lax.all_gather(key_rows, "ctx", axis=0, tiled=True)
    value_piece = lax.all_gather(values, "ctx", axis=0, tiled=True)
    scores = (
        jnp.einsum("hrd,khd->hrk", head_rows, key_piece, preferred_element_type=jnp.float32)
        * inv_root
    )
    key_pos = jnp.arange(key_piece.shape[0], dtype=jnp.int32)
    visible = (key_pos[None, :] <= row_pos[:, None])[None]
    masked = jnp.where(visible, scores, -1e30)
    newest = jnp.maximum(highest, jnp.max(masked, axis=-1))
    weights = jnp.where(visible, jnp.exp(masked - newest[..., None]), 0.0)
    running = jnp.sum(weights, axis=-1)
    summed = jnp.einsum(
        "hrk,khd->hrd",
        weights.astype(jnp.bfloat16),
        value_piece,
        preferred_element_type=jnp.float32,
    )
    highest, running, summed = (newest, running, summed)
    result = (summed / running[..., None]).astype(jnp.bfloat16)
    return jnp.transpose(
        result.reshape(head_count, group_count, query_rows, head_size), (2, 0, 1, 3)
    )


def expert_pass(arrived_rows, expert_gate, expert_down):
    coded_in, scale_in = arrived_rows
    senders, capacity, features = coded_in.shape
    resident = expert_gate.shape[0]
    restored = (
        coded_in.astype(jnp.float32).reshape(senders, capacity, scale_in.shape[2], -1)
        * scale_in.astype(jnp.float32)[..., None]
    ).astype(jnp.bfloat16)
    restored = restored.reshape(senders // resident, resident, capacity, features)
    hidden = jax.nn.silu(
        jnp.einsum("sfcd,fdh->sfch", restored, expert_gate, preferred_element_type=jnp.float32)
    ).astype(jnp.bfloat16)
    result = jnp.einsum(
        "sfch,fhd->sfcd", hidden, expert_down, preferred_element_type=jnp.float32
    ).astype(jnp.bfloat16)
    result = result.reshape(senders, capacity, features)
    return result


def body(queries, key_rows, values, offset, tokens, routes, gate_share, expert_gate, expert_down):
    attended = attention_shard(queries, key_rows, values, offset)
    rows_here, features = tokens.shape
    topk_count = routes.shape[1]
    resident = expert_gate.shape[0]
    ctx_devices = lax.axis_size("ctx")
    ep_devices = lax.axis_size("ep")
    expert_total = ctx_devices * ep_devices * resident
    capacity = min(rows_here, max(2, 5 * rows_here * topk_count // (4 * expert_total)))
    scale_blocks = features // 128
    grouped = tokens.astype(jnp.float32).reshape(rows_here, scale_blocks, 128)
    block_scale = (jnp.max(jnp.abs(grouped), axis=-1) + 1e-06).astype(jnp.bfloat16)
    coded_rows = (
        (grouped / block_scale.astype(jnp.float32)[..., None])
        .astype(jnp.bfloat16)
        .reshape(rows_here, features)
    )
    pair_count = rows_here * topk_count
    chosen = routes.reshape(pair_count)
    onehot = (chosen[:, None] == jnp.arange(expert_total, dtype=jnp.int32)[None, :]).astype(
        jnp.bfloat16
    )
    before_mask = (jnp.arange(pair_count)[:, None] > jnp.arange(pair_count)[None, :]).astype(
        jnp.bfloat16
    )
    earlier = jnp.dot(before_mask, onehot, preferred_element_type=jnp.float32)
    slot_index = jnp.sum(earlier * onehot.astype(jnp.float32), axis=1).astype(jnp.int32)
    target = chosen * capacity + slot_index
    matches = (
        jnp.arange(expert_total * capacity, dtype=jnp.int32)[:, None, None]
        == target.reshape(rows_here, topk_count)[None]
    )
    placing = jnp.sum(matches.astype(jnp.int32), axis=2).astype(jnp.bfloat16)
    outgoing = (
        jnp.dot(placing, coded_rows, preferred_element_type=jnp.float32)
        .astype(jnp.bfloat16)
        .reshape(expert_total, capacity, -1)
    )
    outgoing_scale = (
        jnp.dot(placing, block_scale, preferred_element_type=jnp.float32)
        .astype(jnp.bfloat16)
        .reshape(expert_total, capacity, -1)
    )
    computed = expert_pass(
        (
            lax.all_to_all(outgoing, ("ctx", "ep"), split_axis=0, concat_axis=0, tiled=True),
            lax.all_to_all(outgoing_scale, ("ctx", "ep"), split_axis=0, concat_axis=0, tiled=True),
        ),
        expert_gate,
        expert_down,
    )
    returned = lax.all_to_all(computed, ("ctx", "ep"), split_axis=0, concat_axis=0, tiled=True)
    back_width = returned.shape[-1]
    flat_back = returned.reshape(expert_total * capacity, back_width)
    picked = jnp.take(flat_back, target, axis=0)
    parts_in = lax.all_to_all(
        picked.reshape(pair_count, 1, back_width), "tp", split_axis=2, concat_axis=1, tiled=True
    )
    picked = jnp.sum(parts_in.astype(jnp.float32), axis=1).astype(jnp.bfloat16)
    picked = picked.reshape(rows_here, topk_count, -1)
    shares = gate_share / jnp.sum(gate_share, axis=1, keepdims=True)
    mixture = jnp.sum(shares[..., None] * picked.astype(jnp.float32), axis=1).astype(jnp.bfloat16)
    return (attended, mixture)


def prepare_kernel(tokens_ref, routes_ref, gate_ref, out_ref, *, expert_total):
    rows, features = tokens_ref.shape
    gate = gate_ref[...]
    shares = gate / jnp.sum(gate, axis=0, keepdims=True)
    line = lax.broadcasted_iota(jnp.int32, (TAG, rows), 0)
    expert = lax.rem(line, expert_total)
    dense = jnp.zeros((TAG, rows), jnp.float32)
    for k in range(gate.shape[0]):
        dense += jnp.where(routes_ref[k : k + 1, :] == expert, shares[k : k + 1, :], 0.0)
    high = dense.astype(jnp.bfloat16).astype(jnp.float32)
    tag = jnp.where(line < expert_total, high, jnp.where(line < 2 * expert_total, dense - high, 0.0))
    out_ref[:, features:] = tag.T.astype(jnp.bfloat16)
    for block in range(features // 128):
        cols = slice(block * 128, (block + 1) * 128)
        part = tokens_ref[:, cols].astype(jnp.float32)
        scale = jnp.max(jnp.abs(part), axis=1, keepdims=True) + 1e-06
        scale = scale.astype(jnp.bfloat16).astype(jnp.float32)
        coded = (part / scale).astype(jnp.bfloat16).astype(jnp.float32)
        out_ref[:, cols] = (coded * scale).astype(jnp.bfloat16)


def prepare(tokens, routes, gate_share, expert_total):
    rows, features = tokens.shape
    return pl.pallas_call(
        functools.partial(prepare_kernel, expert_total=expert_total),
        out_shape=jax.ShapeDtypeStruct((rows, features + TAG), jnp.bfloat16),
    )(tokens, routes.T, gate_share.T)


def experts_kernel(ids_ref, *refs, count, expert_total):
    blocks = refs[:count]
    gates, downs = refs[count : count + 2], refs[count + 2 : count + 4]
    outs = refs[count + 4 : 2 * count + 4]
    rows_in, shares_in, hidden = refs[2 * count + 4 :]
    rows, width = blocks[0].shape
    features = width - TAG
    units = gates[0].shape[1]
    up_tile, down_tile = 256, 512
    lane = lax.broadcasted_iota(jnp.int32, (rows, TAG), 1)
    for i, block in enumerate(blocks):
        here = slice(i * rows, (i + 1) * rows)
        rows_in[here, :] = block[:, :features]
        tag = block[:, features:].astype(jnp.float32)
        for j in range(2):
            mine = (lane == ids_ref[j]) | (lane == ids_ref[j] + expert_total)
            share = jnp.sum(jnp.where(mine, tag, 0.0), axis=1, keepdims=True)
            shares_in[j, here, :] = jnp.broadcast_to(share, (rows, TAG))
    for j in range(2):
        for start in range(0, units, up_tile):
            value = jnp.dot(
                rows_in[...],
                gates[j][:, start : start + up_tile],
                preferred_element_type=jnp.float32,
            )
            value = value / (1.0 + jnp.exp(-value)) * shares_in[j, :, :1]
            first = j * units + start
            hidden[:, first : first + up_tile] = value.astype(jnp.bfloat16)
    for start in range(0, features, down_tile):
        cols = slice(start, start + down_tile)
        total = jnp.dot(hidden[:, :units], downs[0][:, cols], preferred_element_type=jnp.float32)
        total += jnp.dot(hidden[:, units:], downs[1][:, cols], preferred_element_type=jnp.float32)
        for i, out in enumerate(outs):
            out[:, cols] = total[i * rows : (i + 1) * rows].astype(jnp.bfloat16)


def experts(ids, blocks, gate_a, gate_b, down_a, down_b, expert_total):
    count = len(blocks)
    rows, width = blocks[0].shape
    features, units = gate_a.shape
    inside = pl.BlockSpec(memory_space=pltpu.VMEM)
    return pl.pallas_call(
        functools.partial(experts_kernel, count=count, expert_total=expert_total),
        in_specs=[pl.BlockSpec(memory_space=pltpu.SMEM)] + [inside] * (count + 4),
        out_specs=[inside] * count,
        out_shape=[jax.ShapeDtypeStruct((rows, features), jnp.bfloat16)] * count,
        scratch_shapes=[
            pltpu.VMEM((count * rows, features), jnp.bfloat16),
            pltpu.VMEM((2, count * rows, TAG), jnp.float32),
            pltpu.VMEM((count * rows, 2 * units), jnp.bfloat16),
        ],
        compiler_params=pltpu.CompilerParams(vmem_limit_bytes=16 * 1024 * 1024),
        cost_estimate=pl.CostEstimate(
            flops=8 * count * rows * features * units,
            bytes_accessed=8 * features * units,
            transcendentals=0,
        ),
    )(ids, *blocks, gate_a, gate_b, down_a, down_b)


def hold_kernel(*refs):
    sources, kept, done = refs[:4], refs[4:8], refs[8]
    copies = [pltpu.make_async_copy(sources[i], kept[i], done.at[i]) for i in range(4)]
    for copy in copies:
        copy.start()
    for copy in copies:
        copy.wait()


def hold(*arrays):
    return pl.pallas_call(
        hold_kernel,
        in_specs=[pl.BlockSpec(memory_space=pltpu.HBM)] * 4,
        out_specs=[pl.BlockSpec(memory_space=pltpu.VMEM)] * 4,
        out_shape=[jax.ShapeDtypeStruct(array.shape, array.dtype) for array in arrays],
        scratch_shapes=[pltpu.SemaphoreType.DMA((4,))],
        compiler_params=pltpu.CompilerParams(vmem_limit_bytes=16 * 1024 * 1024),
    )(*arrays)


def attention_kernel(where_ref, queries_ref, *refs, heads, head_size):
    pieces, out_ref = refs[:-1], refs[-1]
    query_rows, width = queries_ref.shape
    groups = width // (heads * head_size)
    span = pieces[0].shape[0]
    row = lax.broadcasted_iota(jnp.int32, (query_rows, span), 0)
    col = lax.broadcasted_iota(jnp.int32, (query_rows, span), 1)
    seen = [
        jnp.concatenate([where_ref[p] + col <= where_ref[len(pieces)] + row] * groups, axis=0)
        for p in range(len(pieces))
    ]
    for h in range(heads):
        first = h * groups * head_size
        rows = jnp.concatenate(
            [
                queries_ref[:, first + g * head_size : first + (g + 1) * head_size]
                for g in range(groups)
            ],
            axis=0,
        )
        scores = []
        for p, piece in enumerate(pieces):
            keys = piece[:, h * head_size : (h + 1) * head_size]
            value = lax.dot_general(
                rows, keys, (((1,), (1,)), ((), ())), preferred_element_type=jnp.float32
            ) * (1.0 / math.sqrt(head_size))
            scores.append(jnp.where(seen[p], value, -1e30))
        top = scores[0].max(axis=1, keepdims=True)
        for value in scores[1:]:
            top = jnp.maximum(top, value.max(axis=1, keepdims=True))
        running = jnp.zeros_like(top)
        summed = jnp.zeros((rows.shape[0], head_size), jnp.float32)
        for p, piece in enumerate(pieces):
            weights = jnp.where(seen[p], jnp.exp(scores[p] - top), 0.0)
            running += weights.sum(axis=1, keepdims=True)
            content = piece[:, (heads + h) * head_size : (heads + h + 1) * head_size]
            summed += jnp.dot(
                weights.astype(jnp.bfloat16), content, preferred_element_type=jnp.float32
            )
        result = (summed / running).astype(jnp.bfloat16)
        for g in range(groups):
            out_ref[:, first + g * head_size : first + (g + 1) * head_size] = result[
                g * query_rows : (g + 1) * query_rows
            ]


def attention_pieces(queries, pieces, positions, heads, head_size):
    query_rows, width = queries.shape
    inside = pl.BlockSpec(memory_space=pltpu.VMEM)
    return pl.pallas_call(
        functools.partial(attention_kernel, heads=heads, head_size=head_size),
        in_specs=[pl.BlockSpec(memory_space=pltpu.SMEM)] + [inside] * (1 + len(pieces)),
        out_specs=inside,
        out_shape=jax.ShapeDtypeStruct((query_rows, width), jnp.bfloat16),
        cost_estimate=pl.CostEstimate(
            flops=10**9, bytes_accessed=4 * 10**6, transcendentals=0
        ),
    )(positions, queries, *pieces)


NEAR = [(0, 1), (1, 0), (2, 3), (3, 2)]
MIDDLE = [(1, 2), (2, 1)]
OUTWARD = [(1, 0), (2, 3)]
INWARD = [(0, 1), (3, 2)]
ACROSS = [(i, i ^ 2) for i in range(4)]
SIBLING = [(i, i ^ 1) for i in range(4)]


def along_z(array, pairs):
    return lax.ppermute(array, "ctx", pairs)


def across(array):
    return lax.ppermute(array, "ep", ACROSS)


def added(*terms):
    return sum(term.astype(jnp.float32) for term in terms).astype(jnp.bfloat16)


def together(*arrays):
    return lax.optimization_barrier(arrays)


def plane_body(queries, key_rows, values, offset, tokens, routes, gate_share, expert_gate, expert_down):
    expert_total = lax.axis_size("ctx") * lax.axis_size("ep")
    z = lax.axis_index("ctx")
    middle = (z == 1) | (z == 2)
    own_expert = z * lax.axis_size("ep") + lax.axis_index("ep")
    ids = jnp.stack([own_expert, own_expert ^ 1]).astype(jnp.int32)
    span, heads, head_size = key_rows.shape
    query_rows = queries.shape[0]
    places = [z, z ^ 1, z ^ 2, z ^ 3]
    positions = jnp.stack([p * span for p in places] + [offset[0] + z * query_rows])
    gate_a, down_a = expert_gate[0], expert_down[0]
    gate_b = lax.ppermute(gate_a, "ep", SIBLING)
    down_b = lax.ppermute(down_a, "ep", SIBLING)

    def run(*blocks):
        return experts(ids, blocks, gate_a, gate_b, down_a, down_b, expert_total)

    own = prepare(tokens, routes, gate_share, expert_total)
    near = along_z(own, NEAR)
    mid_one = along_z(own, MIDDLE)
    own_x = across(own)
    gate_a, gate_b, down_a, down_b = hold(gate_a, gate_b, down_a, down_b)
    near, mid_one, gate_a, gate_b, down_a, down_b = together(
        near, mid_one, gate_a, gate_b, down_a, down_b
    )

    mid_two = along_z(near, MIDDLE)
    end_one = along_z(mid_one, OUTWARD)
    near_x = across(near)
    part_own, part_own_x, part_near = run(own, own_x, near)
    second = jnp.where(middle, mid_one, end_one)
    second, mid_two, part_own, part_own_x, part_near = together(
        second, mid_two, part_own, part_own_x, part_near
    )

    second_x = across(second)
    end_two = along_z(mid_two, OUTWARD)
    part_near_x, part_second = run(near_x, second)
    third = jnp.where(middle, mid_two, end_two)
    keys = jnp.concatenate([key_rows.reshape(span, -1), values.reshape(span, -1)], axis=1)
    flat = queries.reshape(query_rows, -1)
    third, part_near_x, part_second, keys, flat = together(
        third, part_near_x, part_second, keys, flat
    )

    third_x = across(third)
    pieces = [keys] + [along_z(keys, [(i, i ^ j) for i in range(4)]) for j in (1, 2, 3)]
    part_second_x, part_third = run(second_x, third)
    third_x, part_second_x, part_third, *pieces = together(
        third_x, part_second_x, part_third, *pieces
    )
    (part_third_x,) = run(third_x)

    back_third = across(part_third_x)
    attended = attention_pieces(flat, pieces, positions, heads, head_size).reshape(queries.shape)
    back_third, attended = together(back_third, attended)
    sum_third = added(part_third, back_third)
    back_two = along_z(sum_third, INWARD)
    sum_second = added(part_second, across(part_second_x))
    back_mid_two = along_z(added(sum_third, back_two), MIDDLE)
    back_one = along_z(sum_second, INWARD)
    sum_near = added(part_near, across(part_near_x), back_mid_two)
    back_mid_one = along_z(added(sum_second, back_one), MIDDLE)
    back_near = along_z(sum_near, NEAR)
    mixture = added(part_own, across(part_own_x), back_mid_one, back_near)
    return (attended, mixture)


def solution(mesh):
    plane = dict(mesh.shape)
    plane = plane["ctx"] == 4 and plane["ep"] == 4 and plane["tp"] == 1
    return jax.shard_map(
        plane_body if plane else body,
        mesh=mesh,
        in_specs=(
            P(("rep", "ctx"), "tp", "ep", None),
            P(("rep", "ctx"), "tp", None),
            P(("rep", "ctx"), "tp", None),
            P("rep"),
            P(("rep", "ctx", "ep"), None),
            P(("rep", "ctx", "ep"), None),
            P(("rep", "ctx", "ep"), None),
            P(("ctx", "ep"), None, "tp"),
            P(("ctx", "ep"), "tp", None),
        ),
        out_specs=(P(("rep", "ctx"), "tp", "ep", None), P(("rep", "ctx", "ep"), "tp")),
        check_vma=False,
    )
```

```python
import functools
import math

import jax
import jax.numpy as jnp
from jax import lax
from jax.experimental import pallas as pl
from jax.experimental.pallas import tpu as pltpu
from jax.sharding import PartitionSpec as P

TAG = 128


def attention_shard(queries, key_rows, values, offset):
    query_rows, head_count, group_count, head_size = queries.shape
    inv_root = 1.0 / math.sqrt(head_size)
    query_pos = (
        offset[0] + lax.axis_index("ctx") * query_rows + jnp.arange(query_rows, dtype=jnp.int32)
    )
    row_pos = jnp.tile(query_pos, group_count)
    head_rows = jnp.transpose(queries, (1, 2, 0, 3)).reshape(
        head_count, group_count * query_rows, head_size
    )
    state_shape = (head_count, group_count * query_rows)
    highest = jnp.full(state_shape, -1e30, jnp.float32)
    key_piece = lax.all_gather(key_rows, "ctx", axis=0, tiled=True)
    value_piece = lax.all_gather(values, "ctx", axis=0, tiled=True)
    scores = (
        jnp.einsum("hrd,khd->hrk", head_rows, key_piece, preferred_element_type=jnp.float32)
        * inv_root
    )
    key_pos = jnp.arange(key_piece.shape[0], dtype=jnp.int32)
    visible = (key_pos[None, :] <= row_pos[:, None])[None]
    masked = jnp.where(visible, scores, -1e30)
    newest = jnp.maximum(highest, jnp.max(masked, axis=-1))
    weights = jnp.where(visible, jnp.exp(masked - newest[..., None]), 0.0)
    running = jnp.sum(weights, axis=-1)
    summed = jnp.einsum(
        "hrk,khd->hrd",
        weights.astype(jnp.bfloat16),
        value_piece,
        preferred_element_type=jnp.float32,
    )
    highest, running, summed = (newest, running, summed)
    result = (summed / running[..., None]).astype(jnp.bfloat16)
    return jnp.transpose(
        result.reshape(head_count, group_count, query_rows, head_size), (2, 0, 1, 3)
    )


def expert_pass(arrived_rows, expert_gate, expert_down):
    coded_in, scale_in = arrived_rows
    senders, capacity, features = coded_in.shape
    resident = expert_gate.shape[0]
    restored = (
        coded_in.astype(jnp.float32).reshape(senders, capacity, scale_in.shape[2], -1)
        * scale_in.astype(jnp.float32)[..., None]
    ).astype(jnp.bfloat16)
    restored = restored.reshape(senders // resident, resident, capacity, features)
    hidden = jax.nn.silu(
        jnp.einsum("sfcd,fdh->sfch", restored, expert_gate, preferred_element_type=jnp.float32)
    ).astype(jnp.bfloat16)
    result = jnp.einsum(
        "sfch,fhd->sfcd", hidden, expert_down, preferred_element_type=jnp.float32
    ).astype(jnp.bfloat16)
    result = result.reshape(senders, capacity, features)
    return result


def body(queries, key_rows, values, offset, tokens, routes, gate_share, expert_gate, expert_down):
    attended = attention_shard(queries, key_rows, values, offset)
    rows_here, features = tokens.shape
    topk_count = routes.shape[1]
    resident = expert_gate.shape[0]
    ctx_devices = lax.axis_size("ctx")
    ep_devices = lax.axis_size("ep")
    expert_total = ctx_devices * ep_devices * resident
    capacity = min(rows_here, max(2, 5 * rows_here * topk_count // (4 * expert_total)))
    scale_blocks = features // 128
    grouped = tokens.astype(jnp.float32).reshape(rows_here, scale_blocks, 128)
    block_scale = (jnp.max(jnp.abs(grouped), axis=-1) + 1e-06).astype(jnp.bfloat16)
    coded_rows = (
        (grouped / block_scale.astype(jnp.float32)[..., None])
        .astype(jnp.bfloat16)
        .reshape(rows_here, features)
    )
    pair_count = rows_here * topk_count
    chosen = routes.reshape(pair_count)
    onehot = (chosen[:, None] == jnp.arange(expert_total, dtype=jnp.int32)[None, :]).astype(
        jnp.bfloat16
    )
    before_mask = (jnp.arange(pair_count)[:, None] > jnp.arange(pair_count)[None, :]).astype(
        jnp.bfloat16
    )
    earlier = jnp.dot(before_mask, onehot, preferred_element_type=jnp.float32)
    slot_index = jnp.sum(earlier * onehot.astype(jnp.float32), axis=1).astype(jnp.int32)
    target = chosen * capacity + slot_index
    matches = (
        jnp.arange(expert_total * capacity, dtype=jnp.int32)[:, None, None]
        == target.reshape(rows_here, topk_count)[None]
    )
    placing = jnp.sum(matches.astype(jnp.int32), axis=2).astype(jnp.bfloat16)
    outgoing = (
        jnp.dot(placing, coded_rows, preferred_element_type=jnp.float32)
        .astype(jnp.bfloat16)
        .reshape(expert_total, capacity, -1)
    )
    outgoing_scale = (
        jnp.dot(placing, block_scale, preferred_element_type=jnp.float32)
        .astype(jnp.bfloat16)
        .reshape(expert_total, capacity, -1)
    )
    computed = expert_pass(
        (
            lax.all_to_all(outgoing, ("ctx", "ep"), split_axis=0, concat_axis=0, tiled=True),
            lax.all_to_all(outgoing_scale, ("ctx", "ep"), split_axis=0, concat_axis=0, tiled=True),
        ),
        expert_gate,
        expert_down,
    )
    returned = lax.all_to_all(computed, ("ctx", "ep"), split_axis=0, concat_axis=0, tiled=True)
    back_width = returned.shape[-1]
    flat_back = returned.reshape(expert_total * capacity, back_width)
    picked = jnp.take(flat_back, target, axis=0)
    parts_in = lax.all_to_all(
        picked.reshape(pair_count, 1, back_width), "tp", split_axis=2, concat_axis=1, tiled=True
    )
    picked = jnp.sum(parts_in.astype(jnp.float32), axis=1).astype(jnp.bfloat16)
    picked = picked.reshape(rows_here, topk_count, -1)
    shares = gate_share / jnp.sum(gate_share, axis=1, keepdims=True)
    mixture = jnp.sum(shares[..., None] * picked.astype(jnp.float32), axis=1).astype(jnp.bfloat16)
    return (attended, mixture)


def prepare_kernel(tokens_ref, routes_ref, gate_ref, out_ref, *, expert_total):
    rows, features = tokens_ref.shape
    gate = gate_ref[...]
    shares = gate / jnp.sum(gate, axis=0, keepdims=True)
    line = lax.broadcasted_iota(jnp.int32, (TAG, rows), 0)
    expert = lax.rem(line, expert_total)
    dense = jnp.zeros((TAG, rows), jnp.float32)
    for k in range(gate.shape[0]):
        dense += jnp.where(routes_ref[k : k + 1, :] == expert, shares[k : k + 1, :], 0.0)
    high = dense.astype(jnp.bfloat16).astype(jnp.float32)
    tag = jnp.where(line < expert_total, high, jnp.where(line < 2 * expert_total, dense - high, 0.0))
    out_ref[:, features:] = tag.T.astype(jnp.bfloat16)
    for block in range(features // 128):
        cols = slice(block * 128, (block + 1) * 128)
        part = tokens_ref[:, cols].astype(jnp.float32)
        scale = jnp.max(jnp.abs(part), axis=1, keepdims=True) + 1e-06
        scale = scale.astype(jnp.bfloat16).astype(jnp.float32)
        coded = (part / scale).astype(jnp.bfloat16).astype(jnp.float32)
        out_ref[:, cols] = (coded * scale).astype(jnp.bfloat16)


def prepare(tokens, routes, gate_share, expert_total):
    rows, features = tokens.shape
    return pl.pallas_call(
        functools.partial(prepare_kernel, expert_total=expert_total),
        out_shape=jax.ShapeDtypeStruct((rows, features + TAG), jnp.bfloat16),
        compiler_params=pltpu.CompilerParams(vmem_limit_bytes=8 * 1024 * 1024),
    )(tokens, routes.T, gate_share.T)


def experts_kernel(ids_ref, *refs, count, expert_total):
    blocks = refs[:count]
    gates, downs = refs[count : count + 2]
    outs = refs[count + 2 : 2 * count + 2]
    rows_in, shares_in, hidden = refs[2 * count + 2 :]
    rows, width = blocks[0].shape
    features = width - TAG
    units = gates.shape[2]
    up_tile, down_tile = 256, 512
    lane = lax.broadcasted_iota(jnp.int32, (rows, TAG), 1)
    for i, block in enumerate(blocks):
        here = slice(i * rows, (i + 1) * rows)
        rows_in[here, :] = block[:, :features]
        tag = block[:, features:].astype(jnp.float32)
        for j in range(2):
            mine = (lane == ids_ref[j]) | (lane == ids_ref[j] + expert_total)
            share = jnp.sum(jnp.where(mine, tag, 0.0), axis=1, keepdims=True)
            shares_in[j, here, :] = jnp.broadcast_to(share, (rows, TAG))
    for j in range(2):
        for start in range(0, units, up_tile):
            value = jnp.dot(
                rows_in[...],
                gates[j, :, start : start + up_tile],
                preferred_element_type=jnp.float32,
            )
            value = value / (1.0 + jnp.exp(-value)) * shares_in[j, :, :1]
            first = j * units + start
            hidden[:, first : first + up_tile] = value.astype(jnp.bfloat16)
    for start in range(0, features, down_tile):
        cols = slice(start, start + down_tile)
        total = jnp.dot(hidden[:, :units], downs[0, :, cols], preferred_element_type=jnp.float32)
        total += jnp.dot(hidden[:, units:], downs[1, :, cols], preferred_element_type=jnp.float32)
        for i, out in enumerate(outs):
            out[:, cols] = total[i * rows : (i + 1) * rows].astype(jnp.bfloat16)


def experts(ids, blocks, gates, downs, expert_total, weight):
    count = len(blocks)
    rows, width = blocks[0].shape
    features, units = gates.shape[1:]
    inside = pl.BlockSpec(memory_space=pltpu.VMEM)
    return pl.pallas_call(
        functools.partial(experts_kernel, count=count, expert_total=expert_total),
        in_specs=[pl.BlockSpec(memory_space=pltpu.SMEM)] + [inside] * (count + 2),
        out_specs=[inside] * count,
        out_shape=[jax.ShapeDtypeStruct((rows, features), jnp.bfloat16)] * count,
        scratch_shapes=[
            pltpu.VMEM((count * rows, features), jnp.bfloat16),
            pltpu.VMEM((2, count * rows, TAG), jnp.float32),
            pltpu.VMEM((count * rows, 2 * units), jnp.bfloat16),
        ],
        compiler_params=pltpu.CompilerParams(vmem_limit_bytes=16 * 1024 * 1024),
        cost_estimate=pl.CostEstimate(
            flops=weight * 8 * count * rows * features * units,
            bytes_accessed=8 * features * units,
            transcendentals=0,
        ),
    )(ids, *blocks, gates, downs)


def hold_kernel(*refs):
    sources, kept, done = refs[:4], refs[4:6], refs[6]
    copies = [
        pltpu.make_async_copy(sources[i], kept[i // 2].at[i % 2], done.at[i]) for i in range(4)
    ]
    for copy in copies:
        copy.start()
    for copy in copies:
        copy.wait()


def hold(gate_a, gate_b, down_a, down_b):
    return pl.pallas_call(
        hold_kernel,
        in_specs=[pl.BlockSpec(memory_space=pltpu.HBM)] * 4,
        out_specs=[pl.BlockSpec(memory_space=pltpu.VMEM)] * 2,
        out_shape=[
            jax.ShapeDtypeStruct((2, *array.shape), array.dtype) for array in (gate_a, down_a)
        ],
        scratch_shapes=[pltpu.SemaphoreType.DMA((4,))],
        compiler_params=pltpu.CompilerParams(vmem_limit_bytes=16 * 1024 * 1024),
    )(gate_a, gate_b, down_a, down_b)


def attention_kernel(where_ref, queries_ref, own_ref, mine_ref, other_ref, out_ref, *, heads, head_size):
    query_rows, width = queries_ref.shape
    groups = width // (heads * head_size)
    half = mine_ref.shape[0] // 3
    pieces = [own_ref]
    for ref in (mine_ref, other_ref):
        pieces += [ref.at[pl.ds(i * half, half)] for i in range(3)]
    seen = []
    for p, piece in enumerate(pieces):
        extent = (query_rows, piece.shape[0])
        row = lax.broadcasted_iota(jnp.int32, extent, 0)
        col = lax.broadcasted_iota(jnp.int32, extent, 1)
        mask = where_ref[p] + col <= where_ref[len(pieces)] + row
        seen.append(jnp.concatenate([mask] * groups, axis=0))
    for h in range(heads):
        first = h * groups * head_size
        rows = jnp.concatenate(
            [
                queries_ref[:, first + g * head_size : first + (g + 1) * head_size]
                for g in range(groups)
            ],
            axis=0,
        )
        scores = []
        for p, piece in enumerate(pieces):
            keys = piece[:, h * head_size : (h + 1) * head_size]
            value = lax.dot_general(
                rows, keys, (((1,), (1,)), ((), ())), preferred_element_type=jnp.float32
            ) * (1.0 / math.sqrt(head_size))
            scores.append(jnp.where(seen[p], value, -1e30))
        top = scores[0].max(axis=1, keepdims=True)
        for value in scores[1:]:
            top = jnp.maximum(top, value.max(axis=1, keepdims=True))
        running = jnp.zeros_like(top)
        summed = jnp.zeros((rows.shape[0], head_size), jnp.float32)
        for p, piece in enumerate(pieces):
            weights = jnp.where(seen[p], jnp.exp(scores[p] - top), 0.0)
            running += weights.sum(axis=1, keepdims=True)
            content = piece[:, (heads + h) * head_size : (heads + h + 1) * head_size]
            summed += jnp.dot(
                weights.astype(jnp.bfloat16), content, preferred_element_type=jnp.float32
            )
        result = (summed / running).astype(jnp.bfloat16)
        for g in range(groups):
            out_ref[:, first + g * head_size : first + (g + 1) * head_size] = result[
                g * query_rows : (g + 1) * query_rows
            ]


def attention_pieces(queries, pieces, positions, heads, head_size):
    query_rows, width = queries.shape
    inside = pl.BlockSpec(memory_space=pltpu.VMEM)
    return pl.pallas_call(
        functools.partial(attention_kernel, heads=heads, head_size=head_size),
        in_specs=[pl.BlockSpec(memory_space=pltpu.SMEM)] + [inside] * (1 + len(pieces)),
        out_specs=inside,
        out_shape=jax.ShapeDtypeStruct((query_rows, width), jnp.bfloat16),
        compiler_params=pltpu.CompilerParams(vmem_limit_bytes=12 * 1024 * 1024),
        cost_estimate=pl.CostEstimate(
            flops=10**9, bytes_accessed=4 * 10**6, transcendentals=0
        ),
    )(positions, queries, *pieces)


NEAR = [(0, 1), (1, 0), (2, 3), (3, 2)]
MIDDLE = [(1, 2), (2, 1)]
OUTWARD = [(1, 0), (2, 3)]
INWARD = [(0, 1), (3, 2)]
ACROSS = [(i, i ^ 2) for i in range(4)]
SIBLING = [(i, i ^ 1) for i in range(4)]


def along_z(array, pairs):
    return lax.ppermute(array, "ctx", pairs)


def across(array):
    return lax.ppermute(array, "ep", ACROSS)


def across_at(places, array):
    pairs = [(4 * z + i, 4 * z + j) for z in places for i, j in ACROSS]
    return lax.ppermute(array, ("ctx", "ep"), pairs)


def added(*terms):
    return sum(term.astype(jnp.float32) for term in terms).astype(jnp.bfloat16)


def together(*arrays):
    return lax.optimization_barrier(arrays)


def plane_body(queries, key_rows, values, offset, tokens, routes, gate_share, expert_gate, expert_down):
    expert_total = lax.axis_size("ctx") * lax.axis_size("ep")
    z = lax.axis_index("ctx")
    middle = (z == 1) | (z == 2)
    own_expert = z * lax.axis_size("ep") + lax.axis_index("ep")
    ids = jnp.stack([own_expert, own_expert ^ 1]).astype(jnp.int32)
    span, heads, head_size = key_rows.shape
    query_rows = queries.shape[0]
    core = lax.axis_index("ep") % 2
    half = span // 2
    places = [z * span]
    places += [(z ^ j) * span + core * half for j in (1, 2, 3)]
    places += [(z ^ j) * span + (1 - core) * half for j in (1, 2, 3)]
    positions = jnp.stack(places + [offset[0] + z * query_rows])
    gate_a, down_a = expert_gate[0], expert_down[0]
    gate_b = lax.ppermute(gate_a, "ep", SIBLING)
    down_b = lax.ppermute(down_a, "ep", SIBLING)

    def run(*blocks, weight=1):
        return experts(ids, blocks, gates, downs, expert_total, weight)

    own = prepare(tokens, routes, gate_share, expert_total)
    near = along_z(own, NEAR)
    mid_one = along_z(own, MIDDLE)
    own_x = across(own)
    keys = jnp.concatenate([key_rows.reshape(span, -1), values.reshape(span, -1)], axis=1)
    flat = queries.reshape(query_rows, -1)
    part = jnp.where(core == 0, keys[:half], keys[half:])
    gate_a, keys, part, flat, positions, ids, middle = together(
        gate_a, keys, part, flat, positions, ids, middle
    )
    gates, downs = hold(gate_a, gate_b, down_a, down_b)
    near, mid_one, gates, downs = together(near, mid_one, gates, downs)

    mid_two = along_z(near, MIDDLE)
    end_one = along_z(mid_one, OUTWARD)
    near_x = across(near)
    part_own, part_own_x, part_near = run(own, own_x, near)
    second = jnp.where(middle, mid_one, end_one)
    second, mid_two, part_own, part_own_x, part_near = together(
        second, mid_two, part_own, part_own_x, part_near
    )

    second_x = across(second)
    end_two = along_z(mid_two, OUTWARD)
    part_near_x, part_second = run(near_x, second)
    third = jnp.where(middle, mid_two, end_two)
    third, part_near_x, part_second, keys, part = together(
        third, part_near_x, part_second, keys, part
    )

    third_x = across(third)
    mine = [along_z(part, [(i, i ^ j) for i in range(4)]) for j in (1, 2, 3)]
    part_second_x, part_third = run(second_x, third)
    back_in = along_z(part_third, INWARD)
    back_side = along_z(part_second_x, MIDDLE)
    third_x, part_second_x, part_third, *mine = together(
        third_x, part_second_x, part_third, *mine
    )
    mine = jnp.concatenate(mine, axis=0)
    (part_third_x,) = run(third_x, weight=10)
    part_third_x, part_second_x = together(part_third_x, part_second_x)

    back_far = along_z(part_third_x, [(0, 2), (3, 1)])
    back_third = across_at((1, 2), part_third_x)
    other = lax.ppermute(mine, "ep", SIBLING)
    back_second = across_at((0, 3), part_second_x)
    back_in, back_side, back_far, back_third, flat = together(
        back_in, back_side, back_far, back_third, flat
    )
    back_near_x = across(added(part_near_x, back_far))
    back_mid_two = along_z(added(part_third, back_third, back_in), MIDDLE)
    attended = attention_pieces(flat, [keys, mine, other], positions, heads, head_size).reshape(queries.shape)
    sum_second = added(part_second, back_second)
    back_one = along_z(sum_second, INWARD)
    back_near = along_z(added(part_near, back_near_x, back_mid_two), NEAR)
    back_mid_one = along_z(added(sum_second, back_one), MIDDLE)
    back_own = across(added(part_own_x, back_side))
    terms = [term.astype(jnp.float32) for term in (part_own, back_own, back_mid_one)]
    (gathered,) = together(sum(terms))
    mixture = added(gathered, back_near)
    return (attended, mixture)


def solution(mesh):
    plane = dict(mesh.shape)
    plane = plane["ctx"] == 4 and plane["ep"] == 4 and plane["tp"] == 1
    return jax.shard_map(
        plane_body if plane else body,
        mesh=mesh,
        in_specs=(
            P(("rep", "ctx"), "tp", "ep", None),
            P(("rep", "ctx"), "tp", None),
            P(("rep", "ctx"), "tp", None),
            P("rep"),
            P(("rep", "ctx", "ep"), None),
            P(("rep", "ctx", "ep"), None),
            P(("rep", "ctx", "ep"), None),
            P(("ctx", "ep"), None, "tp"),
            P(("ctx", "ep"), "tp", None),
        ),
        out_specs=(P(("rep", "ctx"), "tp", "ep", None), P(("rep", "ctx", "ep"), "tp")),
        check_vma=False,
    )
```

```python
import functools
import math

import jax
import jax.numpy as jnp
from jax import lax
from jax.experimental import pallas as pl
from jax.experimental.pallas import tpu as pltpu
from jax.sharding import PartitionSpec as P

TAG = 128


def attention_shard(queries, key_rows, values, offset):
    query_rows, head_count, group_count, head_size = queries.shape
    inv_root = 1.0 / math.sqrt(head_size)
    query_pos = (
        offset[0] + lax.axis_index("ctx") * query_rows + jnp.arange(query_rows, dtype=jnp.int32)
    )
    row_pos = jnp.tile(query_pos, group_count)
    head_rows = jnp.transpose(queries, (1, 2, 0, 3)).reshape(
        head_count, group_count * query_rows, head_size
    )
    state_shape = (head_count, group_count * query_rows)
    highest = jnp.full(state_shape, -1e30, jnp.float32)
    key_piece = lax.all_gather(key_rows, "ctx", axis=0, tiled=True)
    value_piece = lax.all_gather(values, "ctx", axis=0, tiled=True)
    scores = (
        jnp.einsum("hrd,khd->hrk", head_rows, key_piece, preferred_element_type=jnp.float32)
        * inv_root
    )
    key_pos = jnp.arange(key_piece.shape[0], dtype=jnp.int32)
    visible = (key_pos[None, :] <= row_pos[:, None])[None]
    masked = jnp.where(visible, scores, -1e30)
    newest = jnp.maximum(highest, jnp.max(masked, axis=-1))
    weights = jnp.where(visible, jnp.exp(masked - newest[..., None]), 0.0)
    running = jnp.sum(weights, axis=-1)
    summed = jnp.einsum(
        "hrk,khd->hrd",
        weights.astype(jnp.bfloat16),
        value_piece,
        preferred_element_type=jnp.float32,
    )
    highest, running, summed = (newest, running, summed)
    result = (summed / running[..., None]).astype(jnp.bfloat16)
    return jnp.transpose(
        result.reshape(head_count, group_count, query_rows, head_size), (2, 0, 1, 3)
    )


def expert_pass(arrived_rows, expert_gate, expert_down):
    coded_in, scale_in = arrived_rows
    senders, capacity, features = coded_in.shape
    resident = expert_gate.shape[0]
    restored = (
        coded_in.astype(jnp.float32).reshape(senders, capacity, scale_in.shape[2], -1)
        * scale_in.astype(jnp.float32)[..., None]
    ).astype(jnp.bfloat16)
    restored = restored.reshape(senders // resident, resident, capacity, features)
    hidden = jax.nn.silu(
        jnp.einsum("sfcd,fdh->sfch", restored, expert_gate, preferred_element_type=jnp.float32)
    ).astype(jnp.bfloat16)
    result = jnp.einsum(
        "sfch,fhd->sfcd", hidden, expert_down, preferred_element_type=jnp.float32
    ).astype(jnp.bfloat16)
    result = result.reshape(senders, capacity, features)
    return result


def body(queries, key_rows, values, offset, tokens, routes, gate_share, expert_gate, expert_down):
    attended = attention_shard(queries, key_rows, values, offset)
    rows_here, features = tokens.shape
    topk_count = routes.shape[1]
    resident = expert_gate.shape[0]
    ctx_devices = lax.axis_size("ctx")
    ep_devices = lax.axis_size("ep")
    expert_total = ctx_devices * ep_devices * resident
    capacity = min(rows_here, max(2, 5 * rows_here * topk_count // (4 * expert_total)))
    scale_blocks = features // 128
    grouped = tokens.astype(jnp.float32).reshape(rows_here, scale_blocks, 128)
    block_scale = (jnp.max(jnp.abs(grouped), axis=-1) + 1e-06).astype(jnp.bfloat16)
    coded_rows = (
        (grouped / block_scale.astype(jnp.float32)[..., None])
        .astype(jnp.bfloat16)
        .reshape(rows_here, features)
    )
    pair_count = rows_here * topk_count
    chosen = routes.reshape(pair_count)
    onehot = (chosen[:, None] == jnp.arange(expert_total, dtype=jnp.int32)[None, :]).astype(
        jnp.bfloat16
    )
    before_mask = (jnp.arange(pair_count)[:, None] > jnp.arange(pair_count)[None, :]).astype(
        jnp.bfloat16
    )
    earlier = jnp.dot(before_mask, onehot, preferred_element_type=jnp.float32)
    slot_index = jnp.sum(earlier * onehot.astype(jnp.float32), axis=1).astype(jnp.int32)
    target = chosen * capacity + slot_index
    matches = (
        jnp.arange(expert_total * capacity, dtype=jnp.int32)[:, None, None]
        == target.reshape(rows_here, topk_count)[None]
    )
    placing = jnp.sum(matches.astype(jnp.int32), axis=2).astype(jnp.bfloat16)
    outgoing = (
        jnp.dot(placing, coded_rows, preferred_element_type=jnp.float32)
        .astype(jnp.bfloat16)
        .reshape(expert_total, capacity, -1)
    )
    outgoing_scale = (
        jnp.dot(placing, block_scale, preferred_element_type=jnp.float32)
        .astype(jnp.bfloat16)
        .reshape(expert_total, capacity, -1)
    )
    computed = expert_pass(
        (
            lax.all_to_all(outgoing, ("ctx", "ep"), split_axis=0, concat_axis=0, tiled=True),
            lax.all_to_all(outgoing_scale, ("ctx", "ep"), split_axis=0, concat_axis=0, tiled=True),
        ),
        expert_gate,
        expert_down,
    )
    returned = lax.all_to_all(computed, ("ctx", "ep"), split_axis=0, concat_axis=0, tiled=True)
    back_width = returned.shape[-1]
    flat_back = returned.reshape(expert_total * capacity, back_width)
    picked = jnp.take(flat_back, target, axis=0)
    parts_in = lax.all_to_all(
        picked.reshape(pair_count, 1, back_width), "tp", split_axis=2, concat_axis=1, tiled=True
    )
    picked = jnp.sum(parts_in.astype(jnp.float32), axis=1).astype(jnp.bfloat16)
    picked = picked.reshape(rows_here, topk_count, -1)
    shares = gate_share / jnp.sum(gate_share, axis=1, keepdims=True)
    mixture = jnp.sum(shares[..., None] * picked.astype(jnp.float32), axis=1).astype(jnp.bfloat16)
    return (attended, mixture)


def prepare_kernel(tokens_ref, routes_ref, gate_ref, out_ref, *, expert_total):
    rows, features = tokens_ref.shape
    gate = gate_ref[...]
    shares = gate / jnp.sum(gate, axis=0, keepdims=True)
    line = lax.broadcasted_iota(jnp.int32, (TAG, rows), 0)
    expert = lax.rem(line, expert_total)
    dense = jnp.zeros((TAG, rows), jnp.float32)
    for k in range(gate.shape[0]):
        dense += jnp.where(routes_ref[k : k + 1, :] == expert, shares[k : k + 1, :], 0.0)
    high = dense.astype(jnp.bfloat16).astype(jnp.float32)
    tag = jnp.where(line < expert_total, high, jnp.where(line < 2 * expert_total, dense - high, 0.0))
    out_ref[:, features:] = tag.T.astype(jnp.bfloat16)
    for block in range(features // 128):
        cols = slice(block * 128, (block + 1) * 128)
        part = tokens_ref[:, cols].astype(jnp.float32)
        scale = jnp.max(jnp.abs(part), axis=1, keepdims=True) + 1e-06
        scale = scale.astype(jnp.bfloat16).astype(jnp.float32)
        coded = (part / scale).astype(jnp.bfloat16).astype(jnp.float32)
        out_ref[:, cols] = (coded * scale).astype(jnp.bfloat16)


def prepare(tokens, routes, gate_share, expert_total):
    rows, features = tokens.shape
    return pl.pallas_call(
        functools.partial(prepare_kernel, expert_total=expert_total),
        out_shape=jax.ShapeDtypeStruct((rows, features + TAG), jnp.bfloat16),
    )(tokens, routes.T, gate_share.T)


def experts_kernel(ids_ref, *refs, count, expert_total):
    blocks = refs[:count]
    gates, downs = refs[count : count + 2]
    outs = refs[count + 2 : 2 * count + 2]
    rows_in, shares_in, hidden = refs[2 * count + 2 :]
    rows, width = blocks[0].shape
    features = width - TAG
    units = gates.shape[2]
    up_tile, down_tile = 256, 512
    lane = lax.broadcasted_iota(jnp.int32, (rows, TAG), 1)
    for i, block in enumerate(blocks):
        here = slice(i * rows, (i + 1) * rows)
        rows_in[here, :] = block[:, :features]
        tag = block[:, features:].astype(jnp.float32)
        for j in range(2):
            mine = (lane == ids_ref[j]) | (lane == ids_ref[j] + expert_total)
            share = jnp.sum(jnp.where(mine, tag, 0.0), axis=1, keepdims=True)
            shares_in[j, here, :] = jnp.broadcast_to(share, (rows, TAG))
    for j in range(2):
        for start in range(0, units, up_tile):
            value = jnp.dot(
                rows_in[...],
                gates[j, :, start : start + up_tile],
                preferred_element_type=jnp.float32,
            )
            value = value / (1.0 + jnp.exp(-value)) * shares_in[j, :, :1]
            first = j * units + start
            hidden[:, first : first + up_tile] = value.astype(jnp.bfloat16)
    for start in range(0, features, down_tile):
        cols = slice(start, start + down_tile)
        total = jnp.dot(hidden[:, :units], downs[0, :, cols], preferred_element_type=jnp.float32)
        total += jnp.dot(hidden[:, units:], downs[1, :, cols], preferred_element_type=jnp.float32)
        for i, out in enumerate(outs):
            out[:, cols] = total[i * rows : (i + 1) * rows].astype(jnp.bfloat16)


def experts(ids, blocks, gates, downs, expert_total, weight):
    count = len(blocks)
    rows, width = blocks[0].shape
    features, units = gates.shape[1:]
    inside = pl.BlockSpec(memory_space=pltpu.VMEM)
    return pl.pallas_call(
        functools.partial(experts_kernel, count=count, expert_total=expert_total),
        in_specs=[pl.BlockSpec(memory_space=pltpu.SMEM)] + [inside] * (count + 2),
        out_specs=[inside] * count,
        out_shape=[jax.ShapeDtypeStruct((rows, features), jnp.bfloat16)] * count,
        scratch_shapes=[
            pltpu.VMEM((count * rows, features), jnp.bfloat16),
            pltpu.VMEM((2, count * rows, TAG), jnp.float32),
            pltpu.VMEM((count * rows, 2 * units), jnp.bfloat16),
        ],
        compiler_params=pltpu.CompilerParams(vmem_limit_bytes=16 * 1024 * 1024),
        cost_estimate=pl.CostEstimate(
            flops=weight * 8 * count * rows * features * units,
            bytes_accessed=8 * features * units,
            transcendentals=0,
        ),
    )(ids, *blocks, gates, downs)


def hold_kernel(*refs):
    sources, kept, done = refs[:4], refs[4:6], refs[6]
    copies = [
        pltpu.make_async_copy(sources[i], kept[i // 2].at[i % 2], done.at[i]) for i in range(4)
    ]
    for copy in copies:
        copy.start()
    for copy in copies:
        copy.wait()


def hold(gate_a, gate_b, down_a, down_b):
    return pl.pallas_call(
        hold_kernel,
        in_specs=[pl.BlockSpec(memory_space=pltpu.HBM)] * 4,
        out_specs=[pl.BlockSpec(memory_space=pltpu.VMEM)] * 2,
        out_shape=[
            jax.ShapeDtypeStruct((2, *array.shape), array.dtype) for array in (gate_a, down_a)
        ],
        scratch_shapes=[pltpu.SemaphoreType.DMA((4,))],
        compiler_params=pltpu.CompilerParams(vmem_limit_bytes=16 * 1024 * 1024),
    )(gate_a, gate_b, down_a, down_b)


def attention_kernel(where_ref, queries_ref, own_ref, mine_ref, other_ref, out_ref, *, heads, head_size):
    query_rows, width = queries_ref.shape
    groups = width // (heads * head_size)
    span = own_ref.shape[0]
    pieces = [own_ref]
    for ref in (mine_ref, other_ref):
        pieces += [ref.at[pl.ds(0, span)], ref.at[pl.ds(span, span // 2)]]
    seen = []
    for p, piece in enumerate(pieces):
        extent = (query_rows, piece.shape[0])
        row = lax.broadcasted_iota(jnp.int32, extent, 0)
        col = lax.broadcasted_iota(jnp.int32, extent, 1)
        mask = where_ref[p] + col <= where_ref[len(pieces)] + row
        seen.append(jnp.concatenate([mask] * groups, axis=0))
    for h in range(heads):
        first = h * groups * head_size
        rows = jnp.concatenate(
            [
                queries_ref[:, first + g * head_size : first + (g + 1) * head_size]
                for g in range(groups)
            ],
            axis=0,
        )
        scores = []
        for p, piece in enumerate(pieces):
            keys = piece[:, h * head_size : (h + 1) * head_size]
            value = lax.dot_general(
                rows, keys, (((1,), (1,)), ((), ())), preferred_element_type=jnp.float32
            ) * (1.0 / math.sqrt(head_size))
            scores.append(jnp.where(seen[p], value, -1e30))
        top = scores[0].max(axis=1, keepdims=True)
        for value in scores[1:]:
            top = jnp.maximum(top, value.max(axis=1, keepdims=True))
        running = jnp.zeros_like(top)
        summed = jnp.zeros((rows.shape[0], head_size), jnp.float32)
        for p, piece in enumerate(pieces):
            weights = jnp.where(seen[p], jnp.exp(scores[p] - top), 0.0)
            running += weights.sum(axis=1, keepdims=True)
            content = piece[:, (heads + h) * head_size : (heads + h + 1) * head_size]
            summed += jnp.dot(
                weights.astype(jnp.bfloat16), content, preferred_element_type=jnp.float32
            )
        result = (summed / running).astype(jnp.bfloat16)
        for g in range(groups):
            out_ref[:, first + g * head_size : first + (g + 1) * head_size] = result[
                g * query_rows : (g + 1) * query_rows
            ]


def attention_pieces(queries, pieces, positions, heads, head_size):
    query_rows, width = queries.shape
    inside = pl.BlockSpec(memory_space=pltpu.VMEM)
    return pl.pallas_call(
        functools.partial(attention_kernel, heads=heads, head_size=head_size),
        in_specs=[pl.BlockSpec(memory_space=pltpu.SMEM)] + [inside] * (1 + len(pieces)),
        out_specs=inside,
        out_shape=jax.ShapeDtypeStruct((query_rows, width), jnp.bfloat16),
        compiler_params=pltpu.CompilerParams(vmem_limit_bytes=12 * 1024 * 1024),
        cost_estimate=pl.CostEstimate(
            flops=10**9, bytes_accessed=4 * 10**6, transcendentals=0
        ),
    )(positions, queries, *pieces)


NEAR = [(0, 1), (1, 0), (2, 3), (3, 2)]
MIDDLE = [(1, 2), (2, 1)]
OUTWARD = [(1, 0), (2, 3)]
INWARD = [(0, 1), (3, 2)]
ACROSS = [(i, i ^ 2) for i in range(4)]
KEYS = [(4 * z + i, 4 * (z ^ (1 + i % 2)) + i) for z in range(4) for i in range(4)]
SIBLING = [(i, i ^ 1) for i in range(4)]


def along_z(array, pairs):
    return lax.ppermute(array, "ctx", pairs)


def across(array):
    return lax.ppermute(array, "ep", ACROSS)


def across_at(places, array):
    pairs = [(4 * z + i, 4 * z + j) for z in places for i, j in ACROSS]
    return lax.ppermute(array, ("ctx", "ep"), pairs)


def added(*terms):
    return sum(term.astype(jnp.float32) for term in terms).astype(jnp.bfloat16)


def together(*arrays):
    return lax.optimization_barrier(arrays)


def plane_body(queries, key_rows, values, offset, tokens, routes, gate_share, expert_gate, expert_down):
    expert_total = lax.axis_size("ctx") * lax.axis_size("ep")
    z = lax.axis_index("ctx")
    middle = (z == 1) | (z == 2)
    own_expert = z * lax.axis_size("ep") + lax.axis_index("ep")
    ids = jnp.stack([own_expert, own_expert ^ 1]).astype(jnp.int32)
    span, heads, head_size = key_rows.shape
    query_rows = queries.shape[0]
    core = lax.axis_index("ep") % 2
    half = span // 2
    places = [z * span, (z ^ (1 + core)) * span, (z ^ 3) * span + core * half]
    places += [(z ^ (2 - core)) * span, (z ^ 3) * span + (1 - core) * half]
    positions = jnp.stack(places + [offset[0] + z * query_rows])
    gate_a, down_a = expert_gate[0], expert_down[0]
    gate_b = lax.ppermute(gate_a, "ep", SIBLING)
    down_b = lax.ppermute(down_a, "ep", SIBLING)

    def run(*blocks, weight=1):
        return experts(ids, blocks, gates, downs, expert_total, weight)

    own = prepare(tokens, routes, gate_share, expert_total)
    near = along_z(own, NEAR)
    mid_one = along_z(own, MIDDLE)
    own_x = across(own)
    keys = jnp.concatenate([key_rows.reshape(span, -1), values.reshape(span, -1)], axis=1)
    flat = queries.reshape(query_rows, -1)
    part = jnp.where(core == 0, keys[:half], keys[half:])
    gate_a, keys, part, flat, positions, ids, middle = together(
        gate_a, keys, part, flat, positions, ids, middle
    )
    gates, downs = hold(gate_a, gate_b, down_a, down_b)
    near, mid_one, gates, downs = together(near, mid_one, gates, downs)

    mid_two = along_z(near, MIDDLE)
    end_one = along_z(mid_one, OUTWARD)
    near_x = across(near)
    part_own, part_own_x, part_near = run(own, own_x, near)
    second = jnp.where(middle, mid_one, end_one)
    second, mid_two, part_own, part_own_x, part_near = together(
        second, mid_two, part_own, part_own_x, part_near
    )

    second_x = across(second)
    end_two = along_z(mid_two, OUTWARD)
    part_near_x, part_second = run(near_x, second)
    third = jnp.where(middle, mid_two, end_two)
    third, part_near_x, part_second, keys, part = together(
        third, part_near_x, part_second, keys, part
    )

    third_x = across(third)
    mine = [
        lax.ppermute(keys, ("ctx", "ep"), KEYS),
        along_z(part, [(i, i ^ 3) for i in range(4)]),
    ]
    part_second_x, part_third = run(second_x, third)
    back_in = along_z(part_third, INWARD)
    back_side = along_z(part_second_x, MIDDLE)
    third_x, part_second_x, part_third, *mine = together(
        third_x, part_second_x, part_third, *mine
    )
    mine = jnp.concatenate(mine, axis=0)
    (part_third_x,) = run(third_x, weight=10)
    part_third_x, part_second_x = together(part_third_x, part_second_x)

    back_far = along_z(part_third_x, [(0, 2), (3, 1)])
    back_third = across_at((1, 2), part_third_x)
    other = lax.ppermute(mine, "ep", SIBLING)
    back_second = across_at((0, 3), part_second_x)
    back_in, back_side, back_far, back_third, flat = together(
        back_in, back_side, back_far, back_third, flat
    )
    back_near_x = across(added(part_near_x, back_far))
    back_mid_two = along_z(added(part_third, back_third, back_in), MIDDLE)
    attended = attention_pieces(flat, [keys, mine, other], positions, heads, head_size).reshape(queries.shape)
    sum_second = added(part_second, back_second)
    back_one = along_z(sum_second, INWARD)
    back_near = along_z(added(part_near, back_near_x, back_mid_two), NEAR)
    back_mid_one = along_z(added(sum_second, back_one), MIDDLE)
    back_own = across(added(part_own_x, back_side))
    terms = [term.astype(jnp.float32) for term in (part_own, back_own, back_mid_one)]
    (gathered,) = together(sum(terms))
    mixture = added(gathered, back_near)
    return (attended, mixture)


def solution(mesh):
    plane = dict(mesh.shape)
    plane = plane["ctx"] == 4 and plane["ep"] == 4 and plane["tp"] == 1
    return jax.shard_map(
        plane_body if plane else body,
        mesh=mesh,
        in_specs=(
            P(("rep", "ctx"), "tp", "ep", None),
            P(("rep", "ctx"), "tp", None),
            P(("rep", "ctx"), "tp", None),
            P("rep"),
            P(("rep", "ctx", "ep"), None),
            P(("rep", "ctx", "ep"), None),
            P(("rep", "ctx", "ep"), None),
            P(("ctx", "ep"), None, "tp"),
            P(("ctx", "ep"), "tp", None),
        ),
        out_specs=(P(("rep", "ctx"), "tp", "ep", None), P(("rep", "ctx", "ep"), "tp")),
        check_vma=False,
    )
```

```python
import functools
import math

import jax
import jax.numpy as jnp
from jax import lax
from jax.experimental import pallas as pl
from jax.experimental.pallas import tpu as pltpu
from jax.sharding import PartitionSpec as P

TAG = 128


def attention_shard(queries, key_rows, values, offset):
    query_rows, head_count, group_count, head_size = queries.shape
    inv_root = 1.0 / math.sqrt(head_size)
    query_pos = (
        offset[0] + lax.axis_index("ctx") * query_rows + jnp.arange(query_rows, dtype=jnp.int32)
    )
    row_pos = jnp.tile(query_pos, group_count)
    head_rows = jnp.transpose(queries, (1, 2, 0, 3)).reshape(
        head_count, group_count * query_rows, head_size
    )
    state_shape = (head_count, group_count * query_rows)
    highest = jnp.full(state_shape, -1e30, jnp.float32)
    key_piece = lax.all_gather(key_rows, "ctx", axis=0, tiled=True)
    value_piece = lax.all_gather(values, "ctx", axis=0, tiled=True)
    scores = (
        jnp.einsum("hrd,khd->hrk", head_rows, key_piece, preferred_element_type=jnp.float32)
        * inv_root
    )
    key_pos = jnp.arange(key_piece.shape[0], dtype=jnp.int32)
    visible = (key_pos[None, :] <= row_pos[:, None])[None]
    masked = jnp.where(visible, scores, -1e30)
    newest = jnp.maximum(highest, jnp.max(masked, axis=-1))
    weights = jnp.where(visible, jnp.exp(masked - newest[..., None]), 0.0)
    running = jnp.sum(weights, axis=-1)
    summed = jnp.einsum(
        "hrk,khd->hrd",
        weights.astype(jnp.bfloat16),
        value_piece,
        preferred_element_type=jnp.float32,
    )
    highest, running, summed = (newest, running, summed)
    result = (summed / running[..., None]).astype(jnp.bfloat16)
    return jnp.transpose(
        result.reshape(head_count, group_count, query_rows, head_size), (2, 0, 1, 3)
    )


def expert_pass(arrived_rows, expert_gate, expert_down):
    coded_in, scale_in = arrived_rows
    senders, capacity, features = coded_in.shape
    resident = expert_gate.shape[0]
    restored = (
        coded_in.astype(jnp.float32).reshape(senders, capacity, scale_in.shape[2], -1)
        * scale_in.astype(jnp.float32)[..., None]
    ).astype(jnp.bfloat16)
    restored = restored.reshape(senders // resident, resident, capacity, features)
    hidden = jax.nn.silu(
        jnp.einsum("sfcd,fdh->sfch", restored, expert_gate, preferred_element_type=jnp.float32)
    ).astype(jnp.bfloat16)
    result = jnp.einsum(
        "sfch,fhd->sfcd", hidden, expert_down, preferred_element_type=jnp.float32
    ).astype(jnp.bfloat16)
    result = result.reshape(senders, capacity, features)
    return result


def body(queries, key_rows, values, offset, tokens, routes, gate_share, expert_gate, expert_down):
    attended = attention_shard(queries, key_rows, values, offset)
    rows_here, features = tokens.shape
    topk_count = routes.shape[1]
    resident = expert_gate.shape[0]
    ctx_devices = lax.axis_size("ctx")
    ep_devices = lax.axis_size("ep")
    expert_total = ctx_devices * ep_devices * resident
    capacity = min(rows_here, max(2, 5 * rows_here * topk_count // (4 * expert_total)))
    scale_blocks = features // 128
    grouped = tokens.astype(jnp.float32).reshape(rows_here, scale_blocks, 128)
    block_scale = (jnp.max(jnp.abs(grouped), axis=-1) + 1e-06).astype(jnp.bfloat16)
    coded_rows = (
        (grouped / block_scale.astype(jnp.float32)[..., None])
        .astype(jnp.bfloat16)
        .reshape(rows_here, features)
    )
    pair_count = rows_here * topk_count
    chosen = routes.reshape(pair_count)
    onehot = (chosen[:, None] == jnp.arange(expert_total, dtype=jnp.int32)[None, :]).astype(
        jnp.bfloat16
    )
    before_mask = (jnp.arange(pair_count)[:, None] > jnp.arange(pair_count)[None, :]).astype(
        jnp.bfloat16
    )
    earlier = jnp.dot(before_mask, onehot, preferred_element_type=jnp.float32)
    slot_index = jnp.sum(earlier * onehot.astype(jnp.float32), axis=1).astype(jnp.int32)
    target = chosen * capacity + slot_index
    matches = (
        jnp.arange(expert_total * capacity, dtype=jnp.int32)[:, None, None]
        == target.reshape(rows_here, topk_count)[None]
    )
    placing = jnp.sum(matches.astype(jnp.int32), axis=2).astype(jnp.bfloat16)
    outgoing = (
        jnp.dot(placing, coded_rows, preferred_element_type=jnp.float32)
        .astype(jnp.bfloat16)
        .reshape(expert_total, capacity, -1)
    )
    outgoing_scale = (
        jnp.dot(placing, block_scale, preferred_element_type=jnp.float32)
        .astype(jnp.bfloat16)
        .reshape(expert_total, capacity, -1)
    )
    computed = expert_pass(
        (
            lax.all_to_all(outgoing, ("ctx", "ep"), split_axis=0, concat_axis=0, tiled=True),
            lax.all_to_all(outgoing_scale, ("ctx", "ep"), split_axis=0, concat_axis=0, tiled=True),
        ),
        expert_gate,
        expert_down,
    )
    returned = lax.all_to_all(computed, ("ctx", "ep"), split_axis=0, concat_axis=0, tiled=True)
    back_width = returned.shape[-1]
    flat_back = returned.reshape(expert_total * capacity, back_width)
    picked = jnp.take(flat_back, target, axis=0)
    parts_in = lax.all_to_all(
        picked.reshape(pair_count, 1, back_width), "tp", split_axis=2, concat_axis=1, tiled=True
    )
    picked = jnp.sum(parts_in.astype(jnp.float32), axis=1).astype(jnp.bfloat16)
    picked = picked.reshape(rows_here, topk_count, -1)
    shares = gate_share / jnp.sum(gate_share, axis=1, keepdims=True)
    mixture = jnp.sum(shares[..., None] * picked.astype(jnp.float32), axis=1).astype(jnp.bfloat16)
    return (attended, mixture)


def prepare_kernel(tokens_ref, routes_ref, gate_ref, out_ref, *, expert_total):
    rows, features = tokens_ref.shape
    gate = gate_ref[...]
    shares = gate / jnp.sum(gate, axis=0, keepdims=True)
    line = lax.broadcasted_iota(jnp.int32, (TAG, rows), 0)
    expert = lax.rem(line, expert_total)
    dense = jnp.zeros((TAG, rows), jnp.float32)
    for k in range(gate.shape[0]):
        dense += jnp.where(routes_ref[k : k + 1, :] == expert, shares[k : k + 1, :], 0.0)
    high = dense.astype(jnp.bfloat16).astype(jnp.float32)
    tag = jnp.where(line < expert_total, high, jnp.where(line < 2 * expert_total, dense - high, 0.0))
    out_ref[:, features:] = tag.T.astype(jnp.bfloat16)
    for block in range(features // 128):
        cols = slice(block * 128, (block + 1) * 128)
        part = tokens_ref[:, cols].astype(jnp.float32)
        scale = jnp.max(jnp.abs(part), axis=1, keepdims=True) + 1e-06
        scale = scale.astype(jnp.bfloat16).astype(jnp.float32)
        coded = (part / scale).astype(jnp.bfloat16).astype(jnp.float32)
        out_ref[:, cols] = (coded * scale).astype(jnp.bfloat16)


def prepare(tokens, routes, gate_share, expert_total):
    rows, features = tokens.shape
    return pl.pallas_call(
        functools.partial(prepare_kernel, expert_total=expert_total),
        out_shape=jax.ShapeDtypeStruct((rows, features + TAG), jnp.bfloat16),
    )(tokens, routes.T, gate_share.T)


def experts_kernel(ids_ref, *refs, count, expert_total):
    blocks = refs[:count]
    gates, downs = refs[count : count + 2]
    outs = refs[count + 2 : 2 * count + 2]
    rows_in, shares_in, hidden = refs[2 * count + 2 :]
    rows, width = blocks[0].shape
    features = width - TAG
    units = gates.shape[2]
    up_tile, down_tile = 256, 512
    lane = lax.broadcasted_iota(jnp.int32, (rows, TAG), 1)
    for i, block in enumerate(blocks):
        here = slice(i * rows, (i + 1) * rows)
        rows_in[here, :] = block[:, :features]
        tag = block[:, features:].astype(jnp.float32)
        for j in range(2):
            mine = (lane == ids_ref[j]) | (lane == ids_ref[j] + expert_total)
            share = jnp.sum(jnp.where(mine, tag, 0.0), axis=1, keepdims=True)
            shares_in[j, here, :] = jnp.broadcast_to(share, (rows, TAG))
    for j in range(2):
        for start in range(0, units, up_tile):
            value = jnp.dot(
                rows_in[...],
                gates[j, :, start : start + up_tile],
                preferred_element_type=jnp.float32,
            )
            value = value / (1.0 + jnp.exp(-value)) * shares_in[j, :, :1]
            first = j * units + start
            hidden[:, first : first + up_tile] = value.astype(jnp.bfloat16)
    for start in range(0, features, down_tile):
        cols = slice(start, start + down_tile)
        total = jnp.dot(hidden[:, :units], downs[0, :, cols], preferred_element_type=jnp.float32)
        total += jnp.dot(hidden[:, units:], downs[1, :, cols], preferred_element_type=jnp.float32)
        for i, out in enumerate(outs):
            out[:, cols] = total[i * rows : (i + 1) * rows].astype(jnp.bfloat16)


def experts(ids, blocks, gates, downs, expert_total, weight):
    count = len(blocks)
    rows, width = blocks[0].shape
    features, units = gates.shape[1:]
    inside = pl.BlockSpec(memory_space=pltpu.VMEM)
    return pl.pallas_call(
        functools.partial(experts_kernel, count=count, expert_total=expert_total),
        in_specs=[pl.BlockSpec(memory_space=pltpu.SMEM)] + [inside] * (count + 2),
        out_specs=[inside] * count,
        out_shape=[jax.ShapeDtypeStruct((rows, features), jnp.bfloat16)] * count,
        scratch_shapes=[
            pltpu.VMEM((count * rows, features), jnp.bfloat16),
            pltpu.VMEM((2, count * rows, TAG), jnp.float32),
            pltpu.VMEM((count * rows, 2 * units), jnp.bfloat16),
        ],
        compiler_params=pltpu.CompilerParams(vmem_limit_bytes=16 * 1024 * 1024),
        cost_estimate=pl.CostEstimate(
            flops=weight * 8 * count * rows * features * units,
            bytes_accessed=8 * features * units,
            transcendentals=0,
        ),
    )(ids, *blocks, gates, downs)


def hold_kernel(*refs):
    sources, kept, done = refs[:4], refs[4:6], refs[6]
    copies = [
        pltpu.make_async_copy(sources[i], kept[i // 2].at[i % 2], done.at[i]) for i in range(4)
    ]
    for copy in copies:
        copy.start()
    for copy in copies:
        copy.wait()


def hold(gate_a, gate_b, down_a, down_b):
    return pl.pallas_call(
        hold_kernel,
        in_specs=[pl.BlockSpec(memory_space=pltpu.HBM)] * 4,
        out_specs=[pl.BlockSpec(memory_space=pltpu.VMEM)] * 2,
        out_shape=[
            jax.ShapeDtypeStruct((2, *array.shape), array.dtype) for array in (gate_a, down_a)
        ],
        scratch_shapes=[pltpu.SemaphoreType.DMA((4,))],
        compiler_params=pltpu.CompilerParams(vmem_limit_bytes=16 * 1024 * 1024),
    )(gate_a, gate_b, down_a, down_b)


def attention_kernel(where_ref, queries_ref, own_ref, mine_ref, other_ref, out_ref, *, heads, head_size):
    query_rows, width = queries_ref.shape
    groups = width // (heads * head_size)
    span = own_ref.shape[0]
    pieces = [own_ref]
    for ref in (mine_ref, other_ref):
        pieces += [ref.at[pl.ds(0, span)], ref.at[pl.ds(span, span // 2)]]
    seen = []
    for p, piece in enumerate(pieces):
        extent = (query_rows, piece.shape[0])
        row = lax.broadcasted_iota(jnp.int32, extent, 0)
        col = lax.broadcasted_iota(jnp.int32, extent, 1)
        mask = where_ref[p] + col <= where_ref[len(pieces)] + row
        seen.append(jnp.concatenate([mask] * groups, axis=0))
    for h in range(heads):
        first = h * groups * head_size
        rows = jnp.concatenate(
            [
                queries_ref[:, first + g * head_size : first + (g + 1) * head_size]
                for g in range(groups)
            ],
            axis=0,
        )
        scores = []
        for p, piece in enumerate(pieces):
            keys = piece[:, h * head_size : (h + 1) * head_size]
            value = lax.dot_general(
                rows, keys, (((1,), (1,)), ((), ())), preferred_element_type=jnp.float32
            ) * (1.0 / math.sqrt(head_size))
            scores.append(jnp.where(seen[p], value, -1e30))
        top = scores[0].max(axis=1, keepdims=True)
        for value in scores[1:]:
            top = jnp.maximum(top, value.max(axis=1, keepdims=True))
        running = jnp.zeros_like(top)
        summed = jnp.zeros((rows.shape[0], head_size), jnp.float32)
        for p, piece in enumerate(pieces):
            weights = jnp.where(seen[p], jnp.exp(scores[p] - top), 0.0)
            running += weights.sum(axis=1, keepdims=True)
            content = piece[:, (heads + h) * head_size : (heads + h + 1) * head_size]
            summed += jnp.dot(
                weights.astype(jnp.bfloat16), content, preferred_element_type=jnp.float32
            )
        result = (summed / running).astype(jnp.bfloat16)
        for g in range(groups):
            out_ref[:, first + g * head_size : first + (g + 1) * head_size] = result[
                g * query_rows : (g + 1) * query_rows
            ]


def attention_pieces(queries, pieces, positions, heads, head_size):
    query_rows, width = queries.shape
    inside = pl.BlockSpec(memory_space=pltpu.VMEM)
    return pl.pallas_call(
        functools.partial(attention_kernel, heads=heads, head_size=head_size),
        in_specs=[pl.BlockSpec(memory_space=pltpu.SMEM)] + [inside] * (1 + len(pieces)),
        out_specs=inside,
        out_shape=jax.ShapeDtypeStruct((query_rows, width), jnp.bfloat16),
        compiler_params=pltpu.CompilerParams(vmem_limit_bytes=12 * 1024 * 1024),
        cost_estimate=pl.CostEstimate(
            flops=10**9, bytes_accessed=4 * 10**6, transcendentals=0
        ),
    )(positions, queries, *pieces)


def combine_kernel(*refs):
    out = refs[-1]
    step = 16
    for first in range(0, out.shape[0], step):
        here = slice(first, first + step)
        total = refs[0][here, :].astype(jnp.float32)
        for ref in refs[1:-1]:
            total += ref[here, :].astype(jnp.float32)
        out[here, :] = total.astype(jnp.bfloat16)


def combined(*terms):
    return pl.pallas_call(
        combine_kernel,
        out_shape=jax.ShapeDtypeStruct(terms[0].shape, jnp.bfloat16),
        compiler_params=pltpu.CompilerParams(vmem_limit_bytes=16 * 1024 * 1024),
    )(*terms)


NEAR = [(0, 1), (1, 0), (2, 3), (3, 2)]
MIDDLE = [(1, 2), (2, 1)]
OUTWARD = [(1, 0), (2, 3)]
INWARD = [(0, 1), (3, 2)]
ACROSS = [(i, i ^ 2) for i in range(4)]
KEYS = [(4 * z + i, 4 * (z ^ (1 + i % 2)) + i) for z in range(4) for i in range(4)]
SIBLING = [(i, i ^ 1) for i in range(4)]


def along_z(array, pairs):
    return lax.ppermute(array, "ctx", pairs)


def across(array):
    return lax.ppermute(array, "ep", ACROSS)


def across_at(places, array):
    pairs = [(4 * z + i, 4 * z + j) for z in places for i, j in ACROSS]
    return lax.ppermute(array, ("ctx", "ep"), pairs)


def added(*terms):
    return sum(term.astype(jnp.float32) for term in terms).astype(jnp.bfloat16)


def together(*arrays):
    return lax.optimization_barrier(arrays)


def plane_body(queries, key_rows, values, offset, tokens, routes, gate_share, expert_gate, expert_down):
    expert_total = lax.axis_size("ctx") * lax.axis_size("ep")
    z = lax.axis_index("ctx")
    middle = (z == 1) | (z == 2)
    own_expert = z * lax.axis_size("ep") + lax.axis_index("ep")
    ids = jnp.stack([own_expert, own_expert ^ 1]).astype(jnp.int32)
    span, heads, head_size = key_rows.shape
    query_rows = queries.shape[0]
    core = lax.axis_index("ep") % 2
    half = span // 2
    places = [z * span, (z ^ (1 + core)) * span, (z ^ 3) * span + core * half]
    places += [(z ^ (2 - core)) * span, (z ^ 3) * span + (1 - core) * half]
    positions = jnp.stack(places + [offset[0] + z * query_rows])
    gate_a, down_a = expert_gate[0], expert_down[0]
    gate_b = lax.ppermute(gate_a, "ep", SIBLING)
    down_b = lax.ppermute(down_a, "ep", SIBLING)

    def run(*blocks, weight=1):
        return experts(ids, blocks, gates, downs, expert_total, weight)

    own = prepare(tokens, routes, gate_share, expert_total)
    near = along_z(own, NEAR)
    mid_one = along_z(own, MIDDLE)
    own_x = across(own)
    keys = jnp.concatenate([key_rows.reshape(span, -1), values.reshape(span, -1)], axis=1)
    flat = queries.reshape(query_rows, -1)
    part = jnp.where(core == 0, keys[:half], keys[half:])
    gate_a, keys, part, flat, positions, ids, middle = together(
        gate_a, keys, part, flat, positions, ids, middle
    )
    gates, downs = hold(gate_a, gate_b, down_a, down_b)
    near, mid_one, gates, downs = together(near, mid_one, gates, downs)

    mid_two = along_z(near, MIDDLE)
    end_one = along_z(mid_one, OUTWARD)
    near_x = across(near)
    part_own, part_own_x, part_near = run(own, own_x, near)
    second = jnp.where(middle, mid_one, end_one)
    second, mid_two, part_own, part_own_x, part_near = together(
        second, mid_two, part_own, part_own_x, part_near
    )

    second_x = across(second)
    end_two = along_z(mid_two, OUTWARD)
    part_near_x, part_second = run(near_x, second)
    third = jnp.where(middle, mid_two, end_two)
    third, part_near_x, part_second, keys, part = together(
        third, part_near_x, part_second, keys, part
    )

    third_x = across(third)
    mine = [
        lax.ppermute(keys, ("ctx", "ep"), KEYS),
        along_z(part, [(i, i ^ 3) for i in range(4)]),
    ]
    part_second_x, part_third = run(second_x, third)
    back_in = along_z(part_third, INWARD)
    back_side = along_z(part_second_x, MIDDLE)
    third_x, part_second_x, part_third, *mine = together(
        third_x, part_second_x, part_third, *mine
    )
    mine = jnp.concatenate(mine, axis=0)
    (part_third_x,) = run(third_x, weight=10)
    part_third_x, part_second_x = together(part_third_x, part_second_x)

    back_far = along_z(part_third_x, [(0, 2), (3, 1)])
    back_third = across_at((1, 2), part_third_x)
    other = lax.ppermute(mine, "ep", SIBLING)
    back_second = across_at((0, 3), part_second_x)
    back_in, back_side, back_far, back_third, flat = together(
        back_in, back_side, back_far, back_third, flat
    )
    back_near_x = across(added(part_near_x, back_far))
    back_mid_two = along_z(added(part_third, back_third, back_in), MIDDLE)
    attended = attention_pieces(flat, [keys, mine, other], positions, heads, head_size).reshape(queries.shape)
    sum_second = added(part_second, back_second)
    back_one = along_z(sum_second, INWARD)
    back_near = along_z(added(part_near, back_near_x, back_mid_two), NEAR)
    back_mid_one = along_z(added(sum_second, back_one), MIDDLE)
    back_own = across(added(part_own_x, back_side))
    terms = [term.astype(jnp.float32) for term in (part_own, back_own, back_mid_one)]
    (gathered,) = together(sum(terms))
    mixture = combined(gathered, back_near)
    return (attended, mixture)


def solution(mesh):
    plane = dict(mesh.shape)
    plane = plane["ctx"] == 4 and plane["ep"] == 4 and plane["tp"] == 1
    return jax.shard_map(
        plane_body if plane else body,
        mesh=mesh,
        in_specs=(
            P(("rep", "ctx"), "tp", "ep", None),
            P(("rep", "ctx"), "tp", None),
            P(("rep", "ctx"), "tp", None),
            P("rep"),
            P(("rep", "ctx", "ep"), None),
            P(("rep", "ctx", "ep"), None),
            P(("rep", "ctx", "ep"), None),
            P(("ctx", "ep"), None, "tp"),
            P(("ctx", "ep"), "tp", None),
        ),
        out_specs=(P(("rep", "ctx"), "tp", "ep", None), P(("rep", "ctx", "ep"), "tp")),
        check_vma=False,
    )
```

```python
import functools
import math

import jax
import jax.numpy as jnp
from jax import lax
from jax.experimental import pallas as pl
from jax.experimental.pallas import tpu as pltpu
from jax.sharding import PartitionSpec as P

TAG = 128


def attention_shard(queries, key_rows, values, offset):
    query_rows, head_count, group_count, head_size = queries.shape
    inv_root = 1.0 / math.sqrt(head_size)
    query_pos = (
        offset[0] + lax.axis_index("ctx") * query_rows + jnp.arange(query_rows, dtype=jnp.int32)
    )
    row_pos = jnp.tile(query_pos, group_count)
    head_rows = jnp.transpose(queries, (1, 2, 0, 3)).reshape(
        head_count, group_count * query_rows, head_size
    )
    state_shape = (head_count, group_count * query_rows)
    highest = jnp.full(state_shape, -1e30, jnp.float32)
    key_piece = lax.all_gather(key_rows, "ctx", axis=0, tiled=True)
    value_piece = lax.all_gather(values, "ctx", axis=0, tiled=True)
    scores = (
        jnp.einsum("hrd,khd->hrk", head_rows, key_piece, preferred_element_type=jnp.float32)
        * inv_root
    )
    key_pos = jnp.arange(key_piece.shape[0], dtype=jnp.int32)
    visible = (key_pos[None, :] <= row_pos[:, None])[None]
    masked = jnp.where(visible, scores, -1e30)
    newest = jnp.maximum(highest, jnp.max(masked, axis=-1))
    weights = jnp.where(visible, jnp.exp(masked - newest[..., None]), 0.0)
    running = jnp.sum(weights, axis=-1)
    summed = jnp.einsum(
        "hrk,khd->hrd",
        weights.astype(jnp.bfloat16),
        value_piece,
        preferred_element_type=jnp.float32,
    )
    highest, running, summed = (newest, running, summed)
    result = (summed / running[..., None]).astype(jnp.bfloat16)
    return jnp.transpose(
        result.reshape(head_count, group_count, query_rows, head_size), (2, 0, 1, 3)
    )


def expert_pass(arrived_rows, expert_gate, expert_down):
    coded_in, scale_in = arrived_rows
    senders, capacity, features = coded_in.shape
    resident = expert_gate.shape[0]
    restored = (
        coded_in.astype(jnp.float32).reshape(senders, capacity, scale_in.shape[2], -1)
        * scale_in.astype(jnp.float32)[..., None]
    ).astype(jnp.bfloat16)
    restored = restored.reshape(senders // resident, resident, capacity, features)
    hidden = jax.nn.silu(
        jnp.einsum("sfcd,fdh->sfch", restored, expert_gate, preferred_element_type=jnp.float32)
    ).astype(jnp.bfloat16)
    result = jnp.einsum(
        "sfch,fhd->sfcd", hidden, expert_down, preferred_element_type=jnp.float32
    ).astype(jnp.bfloat16)
    result = result.reshape(senders, capacity, features)
    return result


def body(queries, key_rows, values, offset, tokens, routes, gate_share, expert_gate, expert_down):
    attended = attention_shard(queries, key_rows, values, offset)
    rows_here, features = tokens.shape
    topk_count = routes.shape[1]
    resident = expert_gate.shape[0]
    ctx_devices = lax.axis_size("ctx")
    ep_devices = lax.axis_size("ep")
    expert_total = ctx_devices * ep_devices * resident
    capacity = min(rows_here, max(2, 5 * rows_here * topk_count // (4 * expert_total)))
    scale_blocks = features // 128
    grouped = tokens.astype(jnp.float32).reshape(rows_here, scale_blocks, 128)
    block_scale = (jnp.max(jnp.abs(grouped), axis=-1) + 1e-06).astype(jnp.bfloat16)
    coded_rows = (
        (grouped / block_scale.astype(jnp.float32)[..., None])
        .astype(jnp.bfloat16)
        .reshape(rows_here, features)
    )
    pair_count = rows_here * topk_count
    chosen = routes.reshape(pair_count)
    onehot = (chosen[:, None] == jnp.arange(expert_total, dtype=jnp.int32)[None, :]).astype(
        jnp.bfloat16
    )
    before_mask = (jnp.arange(pair_count)[:, None] > jnp.arange(pair_count)[None, :]).astype(
        jnp.bfloat16
    )
    earlier = jnp.dot(before_mask, onehot, preferred_element_type=jnp.float32)
    slot_index = jnp.sum(earlier * onehot.astype(jnp.float32), axis=1).astype(jnp.int32)
    target = chosen * capacity + slot_index
    matches = (
        jnp.arange(expert_total * capacity, dtype=jnp.int32)[:, None, None]
        == target.reshape(rows_here, topk_count)[None]
    )
    placing = jnp.sum(matches.astype(jnp.int32), axis=2).astype(jnp.bfloat16)
    outgoing = (
        jnp.dot(placing, coded_rows, preferred_element_type=jnp.float32)
        .astype(jnp.bfloat16)
        .reshape(expert_total, capacity, -1)
    )
    outgoing_scale = (
        jnp.dot(placing, block_scale, preferred_element_type=jnp.float32)
        .astype(jnp.bfloat16)
        .reshape(expert_total, capacity, -1)
    )
    computed = expert_pass(
        (
            lax.all_to_all(outgoing, ("ctx", "ep"), split_axis=0, concat_axis=0, tiled=True),
            lax.all_to_all(outgoing_scale, ("ctx", "ep"), split_axis=0, concat_axis=0, tiled=True),
        ),
        expert_gate,
        expert_down,
    )
    returned = lax.all_to_all(computed, ("ctx", "ep"), split_axis=0, concat_axis=0, tiled=True)
    back_width = returned.shape[-1]
    flat_back = returned.reshape(expert_total * capacity, back_width)
    picked = jnp.take(flat_back, target, axis=0)
    parts_in = lax.all_to_all(
        picked.reshape(pair_count, 1, back_width), "tp", split_axis=2, concat_axis=1, tiled=True
    )
    picked = jnp.sum(parts_in.astype(jnp.float32), axis=1).astype(jnp.bfloat16)
    picked = picked.reshape(rows_here, topk_count, -1)
    shares = gate_share / jnp.sum(gate_share, axis=1, keepdims=True)
    mixture = jnp.sum(shares[..., None] * picked.astype(jnp.float32), axis=1).astype(jnp.bfloat16)
    return (attended, mixture)


def prepare_kernel(tokens_ref, routes_ref, gate_ref, out_ref, *, expert_total):
    rows, features = tokens_ref.shape
    gate = gate_ref[...]
    shares = gate / jnp.sum(gate, axis=0, keepdims=True)
    line = lax.broadcasted_iota(jnp.int32, (TAG, rows), 0)
    expert = lax.rem(line, expert_total)
    dense = jnp.zeros((TAG, rows), jnp.float32)
    for k in range(gate.shape[0]):
        dense += jnp.where(routes_ref[k : k + 1, :] == expert, shares[k : k + 1, :], 0.0)
    high = dense.astype(jnp.bfloat16).astype(jnp.float32)
    tag = jnp.where(line < expert_total, high, jnp.where(line < 2 * expert_total, dense - high, 0.0))
    out_ref[:, features:] = tag.T.astype(jnp.bfloat16)
    for block in range(features // 128):
        cols = slice(block * 128, (block + 1) * 128)
        part = tokens_ref[:, cols].astype(jnp.float32)
        scale = jnp.max(jnp.abs(part), axis=1, keepdims=True) + 1e-06
        scale = scale.astype(jnp.bfloat16).astype(jnp.float32)
        coded = (part / scale).astype(jnp.bfloat16).astype(jnp.float32)
        out_ref[:, cols] = (coded * scale).astype(jnp.bfloat16)


def prepare(tokens, routes, gate_share, expert_total):
    rows, features = tokens.shape
    return pl.pallas_call(
        functools.partial(prepare_kernel, expert_total=expert_total),
        out_shape=jax.ShapeDtypeStruct((rows, features + TAG), jnp.bfloat16),
    )(tokens, routes.T, gate_share.T)


def experts_kernel(ids_ref, *refs, count, expert_total):
    blocks = refs[:count]
    gates, downs = refs[count : count + 2]
    outs = refs[count + 2 : 2 * count + 2]
    rows_in, shares_in, hidden = refs[2 * count + 2 :]
    rows, width = blocks[0].shape
    features = width - TAG
    units = gates.shape[2]
    up_tile, down_tile = 256, 512
    lane = lax.broadcasted_iota(jnp.int32, (rows, TAG), 1)
    for i, block in enumerate(blocks):
        here = slice(i * rows, (i + 1) * rows)
        rows_in[here, :] = block[:, :features]
        tag = block[:, features:].astype(jnp.float32)
        for j in range(2):
            mine = (lane == ids_ref[j]) | (lane == ids_ref[j] + expert_total)
            share = jnp.sum(jnp.where(mine, tag, 0.0), axis=1, keepdims=True)
            shares_in[j, here, :] = jnp.broadcast_to(share, (rows, TAG))
    for j in range(2):
        for start in range(0, units, up_tile):
            value = jnp.dot(
                rows_in[...],
                gates[j, :, start : start + up_tile],
                preferred_element_type=jnp.float32,
            )
            value = value / (1.0 + jnp.exp(-value)) * shares_in[j, :, :1]
            first = j * units + start
            hidden[:, first : first + up_tile] = value.astype(jnp.bfloat16)
    for start in range(0, features, down_tile):
        cols = slice(start, start + down_tile)
        total = jnp.dot(hidden[:, :units], downs[0, :, cols], preferred_element_type=jnp.float32)
        total += jnp.dot(hidden[:, units:], downs[1, :, cols], preferred_element_type=jnp.float32)
        for i, out in enumerate(outs):
            out[:, cols] = total[i * rows : (i + 1) * rows].astype(jnp.bfloat16)


def experts(ids, blocks, gates, downs, expert_total, weight):
    count = len(blocks)
    rows, width = blocks[0].shape
    features, units = gates.shape[1:]
    inside = pl.BlockSpec(memory_space=pltpu.VMEM)
    return pl.pallas_call(
        functools.partial(experts_kernel, count=count, expert_total=expert_total),
        in_specs=[pl.BlockSpec(memory_space=pltpu.SMEM)] + [inside] * (count + 2),
        out_specs=[inside] * count,
        out_shape=[jax.ShapeDtypeStruct((rows, features), jnp.bfloat16)] * count,
        scratch_shapes=[
            pltpu.VMEM((count * rows, features), jnp.bfloat16),
            pltpu.VMEM((2, count * rows, TAG), jnp.float32),
            pltpu.VMEM((count * rows, 2 * units), jnp.bfloat16),
        ],
        compiler_params=pltpu.CompilerParams(vmem_limit_bytes=16 * 1024 * 1024),
        cost_estimate=pl.CostEstimate(
            flops=weight * 8 * count * rows * features * units,
            bytes_accessed=8 * features * units,
            transcendentals=0,
        ),
    )(ids, *blocks, gates, downs)


def hold_kernel(*refs):
    sources, kept, done = refs[:4], refs[4:6], refs[6]
    copies = [
        pltpu.make_async_copy(sources[i], kept[i // 2].at[i % 2], done.at[i]) for i in range(4)
    ]
    for copy in copies:
        copy.start()
    for copy in copies:
        copy.wait()


def hold(gate_a, gate_b, down_a, down_b):
    return pl.pallas_call(
        hold_kernel,
        in_specs=[pl.BlockSpec(memory_space=pltpu.HBM)] * 4,
        out_specs=[pl.BlockSpec(memory_space=pltpu.VMEM)] * 2,
        out_shape=[
            jax.ShapeDtypeStruct((2, *array.shape), array.dtype) for array in (gate_a, down_a)
        ],
        scratch_shapes=[pltpu.SemaphoreType.DMA((4,))],
        compiler_params=pltpu.CompilerParams(vmem_limit_bytes=16 * 1024 * 1024),
    )(gate_a, gate_b, down_a, down_b)


def attention_kernel(where_ref, queries_ref, own_ref, mine_ref, other_ref, out_ref, *, heads, head_size):
    query_rows, width = queries_ref.shape
    groups = width // (heads * head_size)
    span = own_ref.shape[0]
    pieces = [own_ref]
    for ref in (mine_ref, other_ref):
        pieces += [ref.at[pl.ds(0, span)], ref.at[pl.ds(span, span // 2)]]
    seen = []
    for p, piece in enumerate(pieces):
        extent = (query_rows, piece.shape[0])
        row = lax.broadcasted_iota(jnp.int32, extent, 0)
        col = lax.broadcasted_iota(jnp.int32, extent, 1)
        mask = where_ref[p] + col <= where_ref[len(pieces)] + row
        seen.append(jnp.concatenate([mask] * groups, axis=0))
    for h in range(heads):
        first = h * groups * head_size
        rows = jnp.concatenate(
            [
                queries_ref[:, first + g * head_size : first + (g + 1) * head_size]
                for g in range(groups)
            ],
            axis=0,
        )
        scores = []
        for p, piece in enumerate(pieces):
            keys = piece[:, h * head_size : (h + 1) * head_size]
            value = lax.dot_general(
                rows, keys, (((1,), (1,)), ((), ())), preferred_element_type=jnp.float32
            ) * (1.0 / math.sqrt(head_size))
            scores.append(jnp.where(seen[p], value, -1e30))
        top = scores[0].max(axis=1, keepdims=True)
        for value in scores[1:]:
            top = jnp.maximum(top, value.max(axis=1, keepdims=True))
        running = jnp.zeros_like(top)
        summed = jnp.zeros((rows.shape[0], head_size), jnp.float32)
        for p, piece in enumerate(pieces):
            weights = jnp.where(seen[p], jnp.exp(scores[p] - top), 0.0)
            running += weights.sum(axis=1, keepdims=True)
            content = piece[:, (heads + h) * head_size : (heads + h + 1) * head_size]
            summed += jnp.dot(
                weights.astype(jnp.bfloat16), content, preferred_element_type=jnp.float32
            )
        result = (summed / running).astype(jnp.bfloat16)
        for g in range(groups):
            out_ref[:, first + g * head_size : first + (g + 1) * head_size] = result[
                g * query_rows : (g + 1) * query_rows
            ]


def attention_pieces(queries, pieces, positions, heads, head_size):
    query_rows, width = queries.shape
    inside = pl.BlockSpec(memory_space=pltpu.VMEM)
    return pl.pallas_call(
        functools.partial(attention_kernel, heads=heads, head_size=head_size),
        in_specs=[pl.BlockSpec(memory_space=pltpu.SMEM)] + [inside] * (1 + len(pieces)),
        out_specs=inside,
        out_shape=jax.ShapeDtypeStruct((query_rows, width), jnp.bfloat16),
        compiler_params=pltpu.CompilerParams(vmem_limit_bytes=12 * 1024 * 1024),
        cost_estimate=pl.CostEstimate(
            flops=10**9, bytes_accessed=4 * 10**6, transcendentals=0
        ),
    )(positions, queries, *pieces)


def combine_kernel(*refs):
    out = refs[-1]
    step = 16
    for first in range(0, out.shape[0], step):
        here = slice(first, first + step)
        total = refs[0][here, :].astype(jnp.float32)
        for ref in refs[1:-1]:
            total += ref[here, :].astype(jnp.float32)
        out[here, :] = total.astype(jnp.bfloat16)


def combined(*terms):
    return pl.pallas_call(
        combine_kernel,
        out_shape=jax.ShapeDtypeStruct(terms[0].shape, jnp.bfloat16),
        compiler_params=pltpu.CompilerParams(vmem_limit_bytes=16 * 1024 * 1024),
    )(*terms)


NEAR = [(0, 1), (1, 0), (2, 3), (3, 2)]
MIDDLE = [(1, 2), (2, 1)]
OUTWARD = [(1, 0), (2, 3)]
INWARD = [(0, 1), (3, 2)]
ACROSS = [(i, i ^ 2) for i in range(4)]
KEYS = [(4 * z + i, 4 * (z ^ (1 + i % 2)) + i) for z in range(4) for i in range(4)]
SIBLING = [(i, i ^ 1) for i in range(4)]


def along_z(array, pairs):
    return lax.ppermute(array, "ctx", pairs)


def across(array):
    return lax.ppermute(array, "ep", ACROSS)


def across_at(places, array):
    pairs = [(4 * z + i, 4 * z + j) for z in places for i, j in ACROSS]
    return lax.ppermute(array, ("ctx", "ep"), pairs)


def added(*terms):
    return sum(term.astype(jnp.float32) for term in terms).astype(jnp.bfloat16)


def together(*arrays):
    return lax.optimization_barrier(arrays)


def plane_body(queries, key_rows, values, offset, tokens, routes, gate_share, expert_gate, expert_down):
    expert_total = lax.axis_size("ctx") * lax.axis_size("ep")
    z = lax.axis_index("ctx")
    middle = (z == 1) | (z == 2)
    own_expert = z * lax.axis_size("ep") + lax.axis_index("ep")
    ids = jnp.stack([own_expert, own_expert ^ 1]).astype(jnp.int32)
    span, heads, head_size = key_rows.shape
    query_rows = queries.shape[0]
    core = lax.axis_index("ep") % 2
    half = span // 2
    places = [z * span, (z ^ (1 + core)) * span, (z ^ 3) * span + core * half]
    places += [(z ^ (2 - core)) * span, (z ^ 3) * span + (1 - core) * half]
    positions = jnp.stack(places + [offset[0] + z * query_rows])
    gate_a, down_a = expert_gate[0], expert_down[0]
    gate_b = lax.ppermute(gate_a, "ep", SIBLING)
    down_b = lax.ppermute(down_a, "ep", SIBLING)

    def run(*blocks, weight=1):
        return experts(ids, blocks, gates, downs, expert_total, weight)

    own = prepare(tokens, routes, gate_share, expert_total)
    mid_one = along_z(own, MIDDLE)
    near = along_z(own, NEAR)
    own_x = across(own)
    keys = jnp.concatenate([key_rows.reshape(span, -1), values.reshape(span, -1)], axis=1)
    flat = queries.reshape(query_rows, -1)
    part = jnp.where(core == 0, keys[:half], keys[half:])
    gate_a, keys, part, flat, positions, ids, middle = together(
        gate_a, keys, part, flat, positions, ids, middle
    )
    gates, downs = hold(gate_a, gate_b, down_a, down_b)
    mid_one, near, gates, downs = together(mid_one, near, gates, downs)

    mid_two = along_z(near, MIDDLE)
    end_one = along_z(mid_one, OUTWARD)
    near_x = across(near)
    part_own, part_own_x, part_near = run(own, own_x, near)
    second = jnp.where(middle, mid_one, end_one)
    mid_two, second, part_own, part_own_x, part_near = together(
        mid_two, second, part_own, part_own_x, part_near
    )

    second_x = across(second)
    end_two = along_z(mid_two, OUTWARD)
    part_near_x, part_second = run(near_x, second)
    third = jnp.where(middle, mid_two, end_two)
    third, part_near_x, part_second, keys, part = together(
        third, part_near_x, part_second, keys, part
    )

    third_x = across(third)
    mine = [
        lax.ppermute(keys, ("ctx", "ep"), KEYS),
        along_z(part, [(i, i ^ 3) for i in range(4)]),
    ]
    part_second_x, part_third = run(second_x, third)
    back_in = along_z(part_third, INWARD)
    back_side = along_z(part_second_x, MIDDLE)
    third_x, part_second_x, part_third, *mine = together(
        third_x, part_second_x, part_third, *mine
    )
    mine = jnp.concatenate(mine, axis=0)
    (part_third_x,) = run(third_x, weight=10)
    part_third_x, part_second_x = together(part_third_x, part_second_x)

    back_far = along_z(part_third_x, [(0, 2), (3, 1)])
    back_third = across_at((1, 2), part_third_x)
    other = lax.ppermute(mine, "ep", SIBLING)
    back_second = across_at((0, 3), part_second_x)
    back_in, back_side, back_far, back_third, flat = together(
        back_in, back_side, back_far, back_third, flat
    )
    back_near_x = across(added(part_near_x, back_far))
    back_mid_two = along_z(added(part_third, back_third, back_in), MIDDLE)
    attended = attention_pieces(flat, [keys, mine, other], positions, heads, head_size).reshape(queries.shape)
    sum_second = added(part_second, back_second)
    back_one = along_z(sum_second, INWARD)
    back_near = along_z(added(part_near, back_near_x, back_mid_two), NEAR)
    back_mid_one = along_z(added(sum_second, back_one), MIDDLE)
    back_own = across(added(part_own_x, back_side))
    terms = [term.astype(jnp.float32) for term in (part_own, back_own, back_mid_one)]
    (gathered,) = together(sum(terms))
    mixture = combined(gathered, back_near)
    return (attended, mixture)


def solution(mesh):
    plane = dict(mesh.shape)
    plane = plane["ctx"] == 4 and plane["ep"] == 4 and plane["tp"] == 1
    return jax.shard_map(
        plane_body if plane else body,
        mesh=mesh,
        in_specs=(
            P(("rep", "ctx"), "tp", "ep", None),
            P(("rep", "ctx"), "tp", None),
            P(("rep", "ctx"), "tp", None),
            P("rep"),
            P(("rep", "ctx", "ep"), None),
            P(("rep", "ctx", "ep"), None),
            P(("rep", "ctx", "ep"), None),
            P(("ctx", "ep"), None, "tp"),
            P(("ctx", "ep"), "tp", None),
        ),
        out_specs=(P(("rep", "ctx"), "tp", "ep", None), P(("rep", "ctx", "ep"), "tp")),
        check_vma=False,
    )
```
